32 devices in a mesh: outer: 4 (over x, core), inner: 8 (over z, y).
Axes of the slice: x: 2, y: 2, z: 4, core: 2. Of those that a mesh axis runs over, the one named last changes fastest.
Arguments:
- tokens: bfloat16 [512, 3584], P(('outer', 'inner')), may hold values from -6 to 6
- experts: int32 [512, 8], P(('outer', 'inner')), may hold values from 0 to 31, as said below
- gate_score: int32 [512, 8], P(('outer', 'inner')), may hold values from 1 to 16
- expert_gate: bfloat16 [32, 3584, 1024], P(('outer', 'inner')), may hold values from -0.09375 to 0.09375
- expert_up: bfloat16 [32, 3584, 1024], P(('outer', 'inner')), may hold values from -0.09375 to 0.09375
- expert_down: bfloat16 [32, 1024, 3584], P(('outer', 'inner')), may hold values from -0.1875 to 0.1875
- shared_gate: bfloat16 [3584, 2048], P(None, 'inner'), may hold values from -0.09375 to 0.09375
- shared_up: bfloat16 [3584, 2048], P(None, 'inner'), may hold values from -0.09375 to 0.09375
- shared_down: bfloat16 [2048, 3584], P('inner'), may hold values from -0.125 to 0.125
Outputs:
- moe_out: bfloat16 [512, 3584], P(('outer', 'inner'))
The draws below stay inside these ranges and needn't reach their ends.
Inputs may be any that keep to these rules, and one draw needn't show every extreme that they name: Each token names 8 different experts, exactly two in each of 4 different groups, where expert e lies in group e // 8. One group, drawn from the seed, is named by every token. The 16 tokens of one device name one expert at most 4 times, and name each expert of that group exactly 4 times.
All inputs are finite; a program needn't handle non-finite values.
Results may differ from the reference program's by a relative error of at most 0.012.
Values may be sent and summed in bfloat16 or wider, within the bound.
No kernel may reach another device: no remote copies, remote signals or barrier semaphores. Data moves between devices by JAX's collectives and lax.ppermute only.
A program may use at most 128 MiB of HBM per device.

```python
import jax
import jax.numpy as jnp
from jax import lax

D = 3584
FFE = 1024
SHARED_FF = 2048
TOPK = 8
TOP_GROUPS = 4
TOK_DEV = 16
EXPERTS = 32
CAP = 4
TOKENS = 512
N_OUTER = 4
N_INNER = 8


def draw_experts(key, part):
    device_total = N_OUTER * N_INNER
    per_group = TOPK // TOP_GROUPS
    favored = jax.random.randint(jax.random.fold_in(key, 11), (), 0, N_OUTER).astype(jnp.int32)

    def one_device(device_index):
        device_key = jax.random.fold_in(jax.random.fold_in(key, 23), device_index)
        token_keys = jax.random.split(jax.random.fold_in(device_key, 1), TOK_DEV)
        others = jax.vmap(lambda subkey: jax.random.permutation(subkey, N_OUTER - 1))(token_keys)
        others = others[:, :TOP_GROUPS - 1].astype(jnp.int32)
        chosen = jnp.concatenate([jnp.full((TOK_DEV, 1), favored, jnp.int32), (favored + 1 + others) % N_OUTER], axis=1)
        group_keys = jax.random.split(jax.random.fold_in(device_key, 2), N_OUTER)
        shuffled = jax.vmap(lambda subkey: jax.random.permutation(subkey, N_INNER))(group_keys).astype(jnp.int32)
        member = jnp.any(chosen[:, :, None] == jnp.arange(N_OUTER, dtype=jnp.int32)[None, None, :], axis=1).astype(jnp.int32)
        ordinal = jnp.cumsum(member, axis=0) - member
        seen = jnp.take_along_axis(ordinal, chosen, axis=1)
        position = (per_group * seen[:, :, None] + jnp.arange(per_group, dtype=jnp.int32)[None, None, :]) % N_INNER
        local_ids = shuffled[chosen[:, :, None], position]
        ids = (chosen[:, :, None] * N_INNER + local_ids).reshape(TOK_DEV, TOPK)
        slot_keys = jax.random.split(jax.random.fold_in(device_key, 3), TOK_DEV)
        mixing = jax.vmap(lambda subkey: jax.random.permutation(subkey, TOPK))(slot_keys).astype(jnp.int32)
        return jnp.take_along_axis(ids, mixing, axis=1).astype(jnp.int32)
    every = jax.vmap(one_device)(jnp.arange(device_total, dtype=jnp.int32))
    return every.reshape(device_total * TOK_DEV, TOPK)


def place_ends(values, stream_key, smallest, top_value):
    longest = values.shape.index(max(values.shape))
    spots = []
    for shift in (0, 1):
        where = [jax.random.randint(jax.random.fold_in(stream_key, axis), (), 0, length) for axis, length in enumerate(values.shape)]
        where[longest] = (where[longest] + shift) % values.shape[longest]
        spots.append(tuple(where))
    return values.at[spots[0]].set(smallest).at[spots[1]].set(top_value)


def block_scale(stream_key, extent, pieces, low, top_value):
    gain, own = 1.0, jax.random.fold_in(stream_key, 6)
    for axis_at, blocks in pieces:
        heights = jnp.exp(jax.random.uniform(jax.random.fold_in(own, axis_at), (blocks,), jnp.float32, low / len(pieces), top_value / len(pieces)))
        gain = gain * jnp.repeat(heights, extent[axis_at] // blocks).reshape([-1 if axis == axis_at else 1 for axis in range(len(extent))])
    return gain


def scatter_about(key, shape, deviation, bound, cuts=(), kind=jnp.bfloat16):
    entries = deviation * jax.random.normal(key, shape, jnp.float32)
    if cuts:
        entries = entries * block_scale(key, shape, cuts, -0.22, 0.18)
    return jnp.clip(entries, -bound, bound).astype(kind)


def setup_inputs(seed: int = 0) -> dict:
    arg_keys = jax.random.split(jax.random.key(seed), 10)
    tokens = scatter_about(arg_keys[0], (TOKENS, D), 1.0, 6.0, ((0, 32),))
    experts = draw_experts(jax.random.fold_in(arg_keys[9], 71), 0)
    gate_score = place_ends(jax.random.randint(arg_keys[2], (TOKENS, TOPK), 1, 17), jax.random.fold_in(arg_keys[2], 1), 1, 16).astype(jnp.int32)
    expert_gate = scatter_about(arg_keys[3], (EXPERTS, D, FFE), D ** -0.5, 0.09375, ((0, 32),))
    expert_up = scatter_about(arg_keys[4], (EXPERTS, D, FFE), D ** -0.5, 0.09375, ((0, 32),))
    expert_down = scatter_about(arg_keys[5], (EXPERTS, FFE, D), FFE ** -0.5, 0.1875, ((0, 32),))
    shared_gate = scatter_about(arg_keys[6], (D, SHARED_FF), D ** -0.5, 0.09375, ((1, 8),))
    shared_up = scatter_about(arg_keys[7], (D, SHARED_FF), D ** -0.5, 0.09375, ((1, 8),))
    shared_down = scatter_about(arg_keys[8], (SHARED_FF, D), SHARED_FF ** -0.5, 0.125, ((0, 8),))
    return {"tokens": tokens, "experts": experts, "gate_score": gate_score, "expert_gate": expert_gate, "expert_up": expert_up, "expert_down": expert_down, "shared_gate": shared_gate, "shared_up": shared_up, "shared_down": shared_down}


def gated_mlp(inputs, gate_matrix, up_matrix, down_matrix):
    gate_part = jnp.dot(inputs, gate_matrix, preferred_element_type=jnp.float32)
    up_part = jnp.dot(inputs, up_matrix, preferred_element_type=jnp.float32)
    hidden = (jax.nn.silu(gate_part) * up_part).astype(jnp.bfloat16)
    return jnp.dot(hidden, down_matrix, preferred_element_type=jnp.float32).astype(jnp.bfloat16)


def gate_weights(gate_score):
    values = gate_score.astype(jnp.float32)
    return 2.5 * values / jnp.sum(values, axis=-1, keepdims=True)


def group_rank(group_ids):
    slot_width = group_ids.shape[-1]
    same_group = group_ids[..., :, None] == group_ids[..., None, :]
    earlier = jnp.arange(slot_width)[None, :] < jnp.arange(slot_width)[:, None]
    return jnp.sum(jnp.logical_and(same_group, earlier), axis=-1).astype(jnp.int32)


def combine_pairs(pair_rows, pair_weights):
    values = pair_rows.astype(jnp.float32)
    mixed = pair_weights[..., 0, None] * values[..., 0, :] + pair_weights[..., 1, None] * values[..., 1, :]
    return mixed.astype(jnp.bfloat16)


def reference(tokens, experts, gate_score, expert_gate, expert_up, expert_down, shared_gate, shared_up, shared_down):
    token_total = tokens.shape[0]
    device_total = N_OUTER * N_INNER
    per_expert = device_total * CAP
    weights = gate_weights(gate_score)
    blocks = experts.reshape(device_total, TOK_DEV, TOPK)
    expert_ids = jnp.arange(EXPERTS, dtype=jnp.int32)

    def block_ranks(device_block):
        matches = device_block[:, :, None] == expert_ids[None, None, :]
        named_mask = jnp.any(matches, axis=1).astype(jnp.int32)
        earlier = jnp.cumsum(named_mask, axis=0) - named_mask
        return jnp.sum(jnp.where(matches, earlier[:, None, :], 0), axis=2).astype(jnp.int32)

    slot_ranks = jax.vmap(block_ranks)(blocks).reshape(token_total, TOPK)
    device_of = (jnp.arange(token_total, dtype=jnp.int32) // TOK_DEV)[:, None]
    slot_index = (experts * per_expert + device_of * CAP + slot_ranks).astype(jnp.int32)
    owners = jnp.repeat(jnp.arange(token_total, dtype=jnp.int32), TOPK)
    row_table = jnp.full((EXPERTS * per_expert,), token_total, dtype=jnp.int32).at[slot_index.reshape(-1)].set(owners)
    padded = jnp.concatenate([tokens, jnp.zeros((1, D), tokens.dtype)], axis=0)

    def run_expert(operands):
        gate_matrix, up_matrix, down_matrix, expert_rows = operands
        return gated_mlp(padded[expert_rows], gate_matrix, up_matrix, down_matrix)

    outputs = lax.map(run_expert, (expert_gate, expert_up, expert_down, row_table.reshape(EXPERTS, per_expert)))
    flat_rows = outputs.reshape(EXPERTS * per_expert, D)
    group_ids = experts // N_INNER
    slot_rank = group_rank(group_ids)
    routed = jnp.zeros((token_total, D), jnp.float32)
    for group_index in range(N_OUTER):
        pair_rows = []
        pair_weights = []
        for second in range(2):
            picked = jnp.logical_and(group_ids == group_index, slot_rank == second)
            present = jnp.any(picked, axis=1)
            chosen = jnp.sum(jnp.where(picked, slot_index, 0), axis=1).astype(jnp.int32)
            pair_rows.append(jnp.where(present[:, None], flat_rows[chosen], jnp.zeros((), jnp.bfloat16)))
            pair_weights.append(jnp.sum(jnp.where(picked, weights, 0.0), axis=1))
        partial_value = combine_pairs(jnp.stack(pair_rows, axis=1), jnp.stack(pair_weights, axis=1))
        routed = routed + partial_value.astype(jnp.float32)
    gate_part = jnp.dot(tokens, shared_gate, preferred_element_type=jnp.float32)
    up_part = jnp.dot(tokens, shared_up, preferred_element_type=jnp.float32)
    shared_hidden = (jax.nn.silu(gate_part) * up_part).astype(jnp.bfloat16)
    shared = jnp.dot(shared_hidden, shared_down, preferred_element_type=jnp.float32)
    return (shared + routed).astype(jnp.bfloat16)
```

```python
import functools

import jax
import jax.numpy as jnp
from jax import lax
from jax.experimental import pallas as pl
from jax.experimental.pallas import tpu as pltpu
from jax.sharding import PartitionSpec as P

TOPK = 8
TOP_GROUPS = 4
LANES = 128
DEPTH_Z = 4
IN_CUTS = 2
OUT_CUTS = 2
BOTH = ("outer", "inner")
BF16 = jnp.bfloat16
F32 = jnp.float32
PARAMS = pltpu.CompilerParams(vmem_limit_bytes=48 * 1024 * 1024)


def dot(a, b):
    return jnp.dot(a, b, preferred_element_type=F32)


def dot_first(a, b):
    return lax.dot_general(a, b, (((0,), (0,)), ((), ())), preferred_element_type=F32)


def whole(shape, dtype):
    return jax.ShapeDtypeStruct(shape, dtype)


def prepare_kernel(width, tokens_ref, experts_ref, score_ref, *outs):
    names = jnp.concatenate([experts_ref[...], score_ref[...]], axis=0).astype(F32).astype(BF16)
    slots = names.shape[0]
    row = lax.broadcasted_iota(jnp.int32, (slots, LANES), 0)
    col = lax.broadcasted_iota(jnp.int32, (slots, LANES), 1)
    spread = jnp.where(row == col, 1.0, 0.0).astype(BF16)
    for at, out in enumerate(outs):
        out[:, :width] = tokens_ref[:, at * width:(at + 1) * width]
    outs[0][:, width:] = dot_first(names, spread).astype(BF16)


def route_kernel(width, block_rows, capacity, inner_count, blocks, where_ref, *refs):
    pieces, (place_ref, high_ref, low_ref), outs = refs[:blocks], refs[blocks:blocks + 3], refs[blocks + 3:]
    meta = jnp.concatenate([piece[:, width:] for piece in pieces], axis=0).astype(F32)
    token_count = meta.shape[0]
    outer_at, inner_at = where_ref[0], where_ref[1]
    send_rows = inner_count * capacity
    total = send_rows * len(outs)
    slot = lax.broadcasted_iota(jnp.int32, (1, total), 1)
    part = lax.div(slot, jnp.int32(send_rows))
    expert = ((outer_at ^ part) * inner_count + inner_at).astype(F32)
    scores = meta[:, TOPK:2 * TOPK]
    weights = 2.5 * scores / jnp.sum(scores, axis=1, keepdims=True)
    named = jnp.zeros((token_count, total), F32)
    weight = jnp.zeros((token_count, total), F32)
    for k in range(TOPK):
        match = meta[:, k:k + 1] == expert
        named = jnp.where(match, 1.0, named)
        weight = jnp.where(match, weights[:, k:k + 1], weight)
    row = lax.broadcasted_iota(jnp.int32, (token_count, token_count), 0)
    col = lax.broadcasted_iota(jnp.int32, (token_count, token_count), 1)
    rows_each = jnp.int32(block_rows)
    before = jnp.logical_and(lax.div(row, rows_each) == lax.div(col, rows_each), col < row)
    rank = dot(jnp.where(before, 1.0, 0.0).astype(BF16), named.astype(BF16))
    owner = lax.div(lax.broadcasted_iota(jnp.int32, (token_count, 1), 0), rows_each)
    wanted = (slot - part * send_rows - owner * capacity).astype(F32)
    hit = jnp.logical_and(jnp.logical_and(rank == wanted, rank < float(capacity)), named > 0.5)
    place = jnp.where(hit, 1.0, 0.0).astype(BF16)
    place_ref[...] = place
    weight = jnp.where(hit, weight, 0.0)
    high = weight.astype(BF16)
    high_ref[...] = high
    low_ref[...] = (weight - high.astype(F32)).astype(BF16)
    send_selected(width, place, pieces, outs)


def send_selected(width, place, pieces, outs):
    rows = pieces[0].shape[0]
    chosen = sum(
        dot_first(place[at * rows:(at + 1) * rows], piece[:, :width]) for at, piece in enumerate(pieces)
    ).astype(BF16)
    send_rows = outs[0].shape[0]
    for at, out in enumerate(outs):
        out[...] = chosen[at * send_rows:(at + 1) * send_rows]


def select_kernel(width, blocks, place_ref, *refs):
    send_selected(width, place_ref[...], refs[:blocks], refs[blocks:])


def hidden_kernel(blocks, steps, last, *refs):
    pieces = refs[:blocks]
    gate_ref, up_ref = refs[blocks:blocks + 2]
    rest = refs[blocks + 2:]
    step = pl.program_id(0)
    if last:
        gate_in, up_in = rest[:-3] if len(rest) == 5 else (None, None)
        out_ref, gate_sum, up_sum = rest[-3:]
    else:
        gate_in, up_in = rest[:-2] if len(rest) == 4 else (None, None)
        gate_sum, up_sum = rest[-2:]

    @pl.when(step == 0)
    def _():
        if gate_in is None:
            gate_sum[...] = jnp.zeros_like(gate_sum)
            up_sum[...] = jnp.zeros_like(up_sum)
        else:
            gate_sum[...] = gate_in[...]
            up_sum[...] = up_in[...]

    rows = jnp.concatenate([piece[...] for piece in pieces], axis=0)
    gate_sum[...] += dot(rows, gate_ref[...])
    up_sum[...] += dot(rows, up_ref[...])
    if last:

        @pl.when(step == steps - 1)
        def _():
            gate = gate_sum[...]
            out_ref[...] = (gate / (1.0 + jnp.exp(-gate)) * up_sum[...]).astype(BF16)


def hidden(pieces, gate, up, start, width, sums, last):
    blocks = len(pieces)
    token_count = sum(piece.shape[0] for piece in pieces)
    units = gate.shape[1]
    step_width = width // 2 if width // 2 % LANES == 0 else width
    steps = width // step_width
    first = start // step_width
    sum_spec = pl.BlockSpec((token_count, units), lambda s: (0, 0))
    weight_spec = pl.BlockSpec((step_width, units), lambda s: (first + s, 0))
    in_specs = [pl.BlockSpec((piece.shape[0], step_width), lambda s: (0, s)) for piece in pieces]
    in_specs += [weight_spec, weight_spec] + [sum_spec] * len(sums)
    scratch = [pltpu.VMEM((token_count, units), F32)] * 2 if last else []
    if last:
        out_shape, out_specs = whole((token_count, units), BF16), sum_spec
    else:
        out_shape, out_specs = [whole((token_count, units), F32)] * 2, [sum_spec] * 2
    return pl.pallas_call(
        functools.partial(hidden_kernel, blocks, steps, last),
        grid=(steps,),
        in_specs=in_specs,
        out_specs=out_specs,
        out_shape=out_shape,
        scratch_shapes=scratch,
        compiler_params=PARAMS,
    )(*pieces, gate, up, *sums)


def down_kernel(hidden_ref, down_ref, *outs):
    answer = dot(hidden_ref[...], down_ref[...]).astype(BF16)
    rows = outs[0].shape[0]
    for at, out in enumerate(outs):
        out[...] = answer[at * rows:(at + 1) * rows]


def down(rows, matrix, start, width, blocks):
    step_width = width // 2 if width // 2 % LANES == 0 else width
    first = start // step_width
    row_count, units = rows.shape
    each = row_count // blocks
    return pl.pallas_call(
        down_kernel,
        grid=(width // step_width,),
        in_specs=[
            pl.BlockSpec((row_count, units), lambda s: (0, 0)),
            pl.BlockSpec((units, step_width), lambda s: (0, first + s)),
        ],
        out_specs=[pl.BlockSpec((each, step_width), lambda s: (0, s))] * blocks,
        out_shape=[whole((each, width), BF16)] * blocks,
        compiler_params=PARAMS,
    )(rows, matrix)


def combine_kernel(blocks, hidden_ref, down_ref, high_ref, low_ref, *refs):
    answers, keep_ref, outs = refs[:blocks], refs[blocks], refs[blocks + 1:]
    rows = jnp.concatenate([answer[...] for answer in answers], axis=0)
    total = dot(hidden_ref[...], down_ref[...]) + dot(high_ref[...], rows) + dot(low_ref[...], rows)
    each = keep_ref.shape[0]
    keep_ref[...] = total[:each]
    for at, out in enumerate(outs):
        out[...] = total[(at + 1) * each:(at + 2) * each].astype(BF16)


def combine(shared_hidden, shared_down, high, low, answers, start, width, sends):
    token_count, units = shared_hidden.shape
    each = token_count // (sends + 1)
    full = lambda array: pl.BlockSpec(array.shape, lambda s: (0, 0))
    at = start // width
    return pl.pallas_call(
        functools.partial(combine_kernel, len(answers)),
        grid=(1,),
        in_specs=[full(shared_hidden), pl.BlockSpec((units, width), lambda s: (0, at)), full(high), full(low)]
        + [full(answer) for answer in answers],
        out_specs=[pl.BlockSpec((each, width), lambda s: (0, 0))] * (sends + 1),
        out_shape=[whole((each, width), F32)] + [whole((each, width), BF16)] * sends,
        compiler_params=PARAMS,
    )(shared_hidden, shared_down, high, low, *answers)


def add_kernel(blocks, kept_ref, *refs):
    arrived, outs = refs[:blocks], refs[blocks:]
    total = kept_ref[...]
    for block in arrived:
        total = total + block[...].astype(F32)
    each = outs[0].shape[0]
    for at, out in enumerate(outs):
        out[...] = total[at * each:(at + 1) * each].astype(out.dtype)


def finish_kernel(blocks, width, *refs):
    out_ref = refs[-1]
    for at in range((len(refs) - 1) // blocks):
        group = refs[at * blocks:(at + 1) * blocks]
        total = group[0][...]
        for block in group[1:]:
            total = total + block[...].astype(F32)
        out_ref[:, at * width:(at + 1) * width] = total.astype(BF16)


def call(kernel, out_shape, *args, in_specs=None):
    extra = {} if in_specs is None else {"in_specs": in_specs}
    return pl.pallas_call(kernel, out_shape=out_shape, compiler_params=PARAMS, **extra)(*args)


def per_device(
    tokens,
    experts,
    gate_score,
    expert_gate,
    expert_up,
    expert_down,
    shared_gate,
    shared_up,
    shared_down,
):
    rows, model_width = tokens.shape
    inner_count = lax.axis_size("inner")
    outer_count = lax.axis_size("outer")
    depth_y = inner_count // DEPTH_Z
    capacity = TOPK // TOP_GROUPS * rows // inner_count
    send_rows = inner_count * capacity
    device_count = inner_count * outer_count
    where = jnp.stack([lax.axis_index("outer"), lax.axis_index("inner")]).astype(jnp.int32)

    def swap(array, distance):
        return lax.ppermute(array, BOTH, [(at, at ^ distance) for at in range(device_count)])

    def along_z(k):
        return k * depth_y

    def along_outer(k):
        return k * inner_count

    in_width = model_width // IN_CUTS
    out_width = model_width // OUT_CUTS

    sent = call(
        functools.partial(prepare_kernel, in_width),
        [whole((rows, in_width + (LANES if at == 0 else 0)), BF16) for at in range(IN_CUTS)],
        tokens,
        experts.T,
        gate_score.T,
    )
    columns = []
    for piece in sent:
        columns.append(jnp.concatenate([piece] + [swap(piece, along_z(k)) for k in range(1, DEPTH_Z)], axis=0))
    segments = []
    for column in columns:
        segments.append([column] + [swap(column, k) for k in range(1, depth_y)])

    token_count = rows * inner_count
    table = (token_count, device_count * capacity)
    arrived = []
    sums = []
    for at, segment in enumerate(segments):
        send_shapes = [whole((send_rows, in_width), BF16)] * outer_count
        if at == 0:
            place, high, low, *blocks = call(
                functools.partial(route_kernel, in_width, rows, capacity, inner_count, depth_y),
                [whole(table, BF16)] * 3 + send_shapes,
                where,
                *segment,
                in_specs=[pl.BlockSpec(memory_space=pltpu.SMEM)]
                + [pl.BlockSpec(memory_space=pltpu.VMEM)] * depth_y,
            )
        else:
            blocks = call(
                functools.partial(select_kernel, in_width, depth_y), send_shapes, place, *segment
            )
        arrived.append([blocks[0]] + [swap(blocks[k], along_outer(k)) for k in range(1, outer_count)])
    shared_sums = []
    for at, segment in enumerate(segments):
        shared_sums = hidden(
            segment, shared_gate, shared_up, at * in_width, in_width, shared_sums, at == IN_CUTS - 1
        )
    shared_hidden = shared_sums
    for at, blocks in enumerate(arrived):
        sums = hidden(
            blocks, expert_gate[0], expert_up[0], at * in_width, in_width, sums, at == IN_CUTS - 1
        )
    expert_hidden = sums

    finals = []
    for at in range(OUT_CUTS):
        start = at * out_width
        blocks = down(expert_hidden, expert_down[0], start, out_width, outer_count)
        answers = [blocks[0]] + [swap(blocks[k], along_outer(k)) for k in range(1, outer_count)]
        kept, *leaving = combine(
            shared_hidden, shared_down, high, low, answers, start, out_width, depth_y - 1
        )
        coming = [swap(block, k + 1) for k, block in enumerate(leaving)]
        kept, *leaving = call(
            functools.partial(add_kernel, depth_y - 1),
            [whole((rows, out_width), F32)] + [whole((rows, out_width), BF16)] * (DEPTH_Z - 1),
            kept,
            *coming,
        )
        finals += [kept] + [swap(block, along_z(k + 1)) for k, block in enumerate(leaving)]
    return call(
        functools.partial(finish_kernel, DEPTH_Z, out_width), whole((rows, model_width), BF16), *finals
    )


def solution(mesh):
    return jax.shard_map(
        per_device,
        mesh=mesh,
        in_specs=(
            P(("outer", "inner"), None),
            P(("outer", "inner"), None),
            P(("outer", "inner"), None),
            P(("outer", "inner"), None, None),
            P(("outer", "inner"), None, None),
            P(("outer", "inner"), None, None),
            P(None, "inner"),
            P(None, "inner"),
            P("inner", None),
        ),
        out_specs=P(("outer", "inner"), None),
        check_vma=False,
    )
```

```python
import functools

import jax
import jax.numpy as jnp
from jax import lax
from jax.experimental import pallas as pl
from jax.experimental.pallas import tpu as pltpu
from jax.sharding import PartitionSpec as P

TOPK = 8
TOP_GROUPS = 4
LANES = 128
CORES = 2
DEPTH_Z = 4
OUT_CUTS = 2
BOTH = ("outer", "inner")
BF16 = jnp.bfloat16
F32 = jnp.float32
PARAMS = pltpu.CompilerParams(vmem_limit_bytes=16 * 1024 * 1024)
IN_VMEM = pl.BlockSpec(memory_space=pltpu.VMEM)
IN_SMEM = pl.BlockSpec(memory_space=pltpu.SMEM)
ANYWHERE = pl.BlockSpec(memory_space=pl.ANY)


def dot(a, b):
    return jnp.dot(a, b, preferred_element_type=F32)


def dot_first(a, b):
    return lax.dot_general(a, b, (((0,), (0,)), ((), ())), preferred_element_type=F32)


def whole(shape, dtype):
    return jax.ShapeDtypeStruct(shape, dtype)


def call(kernel, out_shape, *args, **more):
    return pl.pallas_call(kernel, out_shape=out_shape, compiler_params=PARAMS, **more)(*args)


def prefetch_kernel(*refs):
    count = (len(refs) - 2) // 2
    token_ref, sem = refs[-2:]
    copies = [
        pltpu.make_async_copy(refs[at], refs[count + at], sem.at[at]) for at in range(count)
    ]
    for copy in copies:
        copy.start()
    token_ref[...] = jnp.zeros_like(token_ref)
    for copy in copies:
        copy.wait()


def far(array):
    return pltpu.with_memory_space_constraint(array, pltpu.HBM)


def after(array, *others):
    return lax.optimization_barrier((array, *others))[0]


def prefetch(*arrays):
    arrays = [far(array) for array in arrays]
    return call(
        prefetch_kernel,
        [pltpu.VMEM(array.shape, array.dtype) for array in arrays] + [pltpu.VMEM((8, LANES), F32)],
        *arrays,
        in_specs=[ANYWHERE] * len(arrays),
        out_specs=[IN_VMEM] * (len(arrays) + 1),
        scratch_shapes=[pltpu.SemaphoreType.DMA((len(arrays),))],
    )


def prepare_kernel(tokens_ref, experts_ref, score_ref, out_ref, experts, scores, sem):
    width = tokens_ref.shape[1]
    copies = [
        pltpu.make_async_copy(experts_ref, experts, sem.at[0]),
        pltpu.make_async_copy(score_ref, scores, sem.at[1]),
        pltpu.make_async_copy(tokens_ref, out_ref.at[:, pl.ds(0, width)], sem.at[2]),
    ]
    for copy in copies:
        copy.start()
    copies[0].wait()
    copies[1].wait()
    names = jnp.concatenate([experts[...], scores[...]], axis=0).astype(F32).astype(BF16)
    slots = names.shape[0]
    row = lax.broadcasted_iota(jnp.int32, (slots, LANES), 0)
    col = lax.broadcasted_iota(jnp.int32, (slots, LANES), 1)
    spread = jnp.where(row == col, 1.0, 0.0).astype(BF16)
    out_ref[:, width:] = dot_first(names, spread).astype(BF16)
    copies[2].wait()


def prepare(tokens, experts, gate_score):
    rows, width = tokens.shape
    return call(
        prepare_kernel,
        pltpu.VMEM((rows, width + LANES), BF16),
        far(tokens),
        far(experts.T),
        far(gate_score.T),
        in_specs=[ANYWHERE] * 3,
        out_specs=IN_VMEM,
        scratch_shapes=[pltpu.VMEM((TOPK, rows), jnp.int32)] * 2 + [pltpu.SemaphoreType.DMA((3,))],
    )


def routing(meta, block_rows, capacity, group_count, expert_of):
    token_count = meta.shape[0]
    send_rows = token_count // block_rows * capacity
    total = send_rows * group_count
    slot = lax.broadcasted_iota(jnp.int32, (1, total), 1)
    group = lax.div(slot, jnp.int32(send_rows))
    expert = expert_of(group).astype(F32)
    scores = meta[:, TOPK:2 * TOPK]
    weights = 2.5 * scores / jnp.sum(scores, axis=1, keepdims=True)
    named = jnp.zeros((token_count, total), F32)
    weight = jnp.zeros((token_count, total), F32)
    for k in range(TOPK):
        match = meta[:, k:k + 1] == expert
        named = jnp.where(match, 1.0, named)
        weight = jnp.where(match, weights[:, k:k + 1], weight)
    row = lax.broadcasted_iota(jnp.int32, (token_count, token_count), 0)
    col = lax.broadcasted_iota(jnp.int32, (token_count, token_count), 1)
    rows_each = jnp.int32(block_rows)
    before = jnp.logical_and(lax.div(row, rows_each) == lax.div(col, rows_each), col < row)
    rank = dot(jnp.where(before, 1.0, 0.0).astype(BF16), named.astype(BF16))
    owner = lax.div(lax.broadcasted_iota(jnp.int32, (token_count, 1), 0), rows_each)
    wanted = (slot - group * send_rows - owner * capacity).astype(F32)
    hit = jnp.logical_and(jnp.logical_and(rank == wanted, rank < float(capacity)), named > 0.5)
    return hit, weight


def select_kernel(width, block_rows, capacity, inner_count, chips_x, blocks, where_ref, *refs):
    pieces, outs = refs[:blocks], refs[blocks + 1:]
    outer_at, inner_at = where_ref[0], where_ref[1]

    def expert_of(group):
        along_y = lax.div(group, jnp.int32(chips_x))
        along_x = group - along_y * chips_x
        return (outer_at ^ (along_x * CORES)) * inner_count + (inner_at ^ along_y)

    meta = jnp.concatenate([piece[:, width:] for piece in pieces], axis=0).astype(F32)
    hit, _ = routing(meta, block_rows, capacity, len(outs), expert_of)
    rows = jnp.concatenate([piece[:, :width] for piece in pieces], axis=0)
    chosen = dot_first(jnp.where(hit, 1.0, 0.0).astype(BF16), rows).astype(BF16)
    each = outs[0].shape[0]
    for at, out in enumerate(outs):
        out[...] = chosen[at * each:(at + 1) * each]


def hidden_kernel(width, blocks, *refs):
    pieces = refs[:blocks]
    gate_ref, up_ref, out_ref = refs[blocks:]
    rows = jnp.concatenate([piece[:, :width] for piece in pieces], axis=0)
    gate = dot(rows, gate_ref[...])
    up = dot(rows, up_ref[...])
    out_ref[...] = (gate / (1.0 + jnp.exp(-gate)) * up).astype(BF16)


def hidden(pieces, gate, up):
    shape = (sum(piece.shape[0] for piece in pieces), gate.shape[1])
    return call(
        functools.partial(hidden_kernel, gate.shape[0], len(pieces)),
        whole(shape, BF16),
        *pieces,
        gate,
        up,
    )


def down_kernel(start, width, chips_x, depth_y, hidden_ref, down_ref, *outs):
    answer = dot(hidden_ref[...], down_ref[:, start:start + width])
    part = outs[0].shape[0] // depth_y
    for at, out in enumerate(outs):
        along_x, core = at // CORES, at % CORES
        firsts = [((y * chips_x + along_x) * CORES + core) * part for y in range(depth_y)]
        out[...] = jnp.concatenate([answer[first:first + part] for first in firsts], axis=0).astype(BF16)


def down(rows, matrix, start, width, outer_count, depth_y):
    return call(
        functools.partial(down_kernel, start, width, outer_count // CORES, depth_y),
        [whole((rows.shape[0] // outer_count, width), BF16)] * outer_count,
        rows,
        matrix,
    )


def table_kernel(width, block_rows, capacity, inner_count, group_count, blocks, where_ref, *refs):
    pieces, (high_ref, low_ref) = refs[:blocks], refs[blocks:]
    outer_at, inner_at = where_ref[0], where_ref[1]
    meta = jnp.concatenate([piece[:, width:] for piece in pieces], axis=0).astype(F32)
    hit, weight = routing(
        meta, block_rows, capacity, group_count, lambda group: (outer_at ^ group) * inner_count + inner_at
    )
    weight = jnp.where(hit, weight, 0.0)
    high = weight.astype(BF16)
    high_ref[...] = high
    low_ref[...] = (weight - high.astype(F32)).astype(BF16)


def combine_kernel(blocks, start, width, hidden_ref, down_ref, high_ref, low_ref, *refs):
    answers, keep_ref, outs = refs[:blocks], refs[blocks], refs[blocks + 1:]
    rows = jnp.concatenate([answer[...] for answer in answers], axis=0)
    total = dot(hidden_ref[...], down_ref[:, start:start + width])
    total = total + dot(high_ref[...], rows) + dot(low_ref[...], rows)
    each = keep_ref.shape[0]
    keep_ref[...] = total[:each]
    for at, out in enumerate(outs):
        out[...] = total[(at + 1) * each:(at + 2) * each].astype(BF16)


def combine(shared_hidden, shared_down, high, low, answers, start, width, sends):
    each = shared_hidden.shape[0] // (sends + 1)
    return call(
        functools.partial(combine_kernel, len(answers), start, width),
        [whole((each, width), F32)] + [whole((each, width), BF16)] * sends,
        shared_hidden,
        shared_down,
        high,
        low,
        *answers,
    )


def add_kernel(blocks, kept_ref, *refs):
    arrived, outs = refs[:blocks], refs[blocks:]
    total = kept_ref[...]
    for block in arrived:
        total = total + block[...].astype(F32)
    each = outs[0].shape[0]
    for at, out in enumerate(outs):
        out[...] = total[at * each:(at + 1) * each].astype(out.dtype)


def finish_kernel(blocks, width, *refs):
    out_ref = refs[-1]
    for at in range((len(refs) - 1) // blocks):
        group = refs[at * blocks:(at + 1) * blocks]
        total = group[0][...]
        for block in group[1:]:
            total = total + block[...].astype(F32)
        out_ref[:, at * width:(at + 1) * width] = total.astype(BF16)


def per_device(
    tokens,
    experts,
    gate_score,
    expert_gate,
    expert_up,
    expert_down,
    shared_gate,
    shared_up,
    shared_down,
):
    rows, model_width = tokens.shape
    inner_count = lax.axis_size("inner")
    outer_count = lax.axis_size("outer")
    depth_y = inner_count // DEPTH_Z
    chips_x = outer_count // CORES
    capacity = TOPK // TOP_GROUPS * rows // inner_count
    device_count = inner_count * outer_count
    where = jnp.stack([lax.axis_index("outer"), lax.axis_index("inner")]).astype(jnp.int32)

    def swap(array, distance):
        return lax.ppermute(array, BOTH, [(at, at ^ distance) for at in range(device_count)])

    def along_z(k):
        return k * depth_y

    def along_outer(k):
        return k * inner_count

    sent = prepare(tokens, experts, gate_score)
    *expert_weights, loaded = prefetch(expert_gate[0], expert_up[0], expert_down[0])
    column = [sent] + [swap(sent, along_z(k)) for k in range(1, DEPTH_Z)]
    *column, loaded = lax.optimization_barrier((*column, loaded))
    at_hand = column + [swap(block, along_outer(1)) for block in column]

    groups = depth_y * chips_x
    blocks = call(
        functools.partial(
            select_kernel, model_width, rows, capacity, inner_count, chips_x, len(at_hand)
        ),
        [whole((CORES * DEPTH_Z * capacity, model_width), BF16)] * groups,
        where,
        *at_hand,
        loaded,
        in_specs=[IN_SMEM] + [IN_VMEM] * len(at_hand) + [ANYWHERE],
    )
    arrived = [blocks[0]]
    for at in range(1, groups):
        along_y, along_x = at // chips_x, at % chips_x
        arrived.append(swap(blocks[at], along_y + along_outer(along_x * CORES)))
    expert_hidden = hidden(arrived, *expert_weights[:2])

    *shared_weights, _ = prefetch(shared_gate, shared_up, shared_down)
    dense = after(jnp.concatenate(column, axis=0), *arrived)
    segment = [dense] + [swap(dense, k) for k in range(1, depth_y)]
    high, low = call(
        functools.partial(
            table_kernel, model_width, rows, capacity, inner_count, outer_count, len(segment)
        ),
        [whole((rows * inner_count, device_count * capacity), BF16)] * 2,
        where,
        *segment,
        in_specs=[IN_SMEM] + [IN_VMEM] * len(segment),
    )
    shared_hidden = hidden(segment, *shared_weights[:2])

    out_width = model_width // OUT_CUTS
    finals = []
    for at in range(OUT_CUTS):
        start = at * out_width
        blocks = down(expert_hidden, expert_weights[2], start, out_width, outer_count, depth_y)
        answers = [blocks[0]] + [swap(blocks[k], along_outer(k)) for k in range(1, outer_count)]
        kept, *leaving = combine(
            shared_hidden, shared_weights[2], high, low, answers, start, out_width, depth_y - 1
        )
        coming = [swap(block, k + 1) for k, block in enumerate(leaving)]
        kept, *leaving = call(
            functools.partial(add_kernel, depth_y - 1),
            [whole((rows, out_width), F32)] + [whole((rows, out_width), BF16)] * (DEPTH_Z - 1),
            kept,
            *coming,
        )
        finals += [kept] + [swap(block, along_z(k + 1)) for k, block in enumerate(leaving)]
    return call(
        functools.partial(finish_kernel, DEPTH_Z, out_width), whole((rows, model_width), BF16), *finals
    )


def solution(mesh):
    return jax.shard_map(
        per_device,
        mesh=mesh,
        in_specs=(
            P(("outer", "inner"), None),
            P(("outer", "inner"), None),
            P(("outer", "inner"), None),
            P(("outer", "inner"), None, None),
            P(("outer", "inner"), None, None),
            P(("outer", "inner"), None, None),
            P(None, "inner"),
            P(None, "inner"),
            P("inner", None),
        ),
        out_specs=P(("outer", "inner"), None),
        check_vma=False,
    )
```

```python
import functools

import jax
import jax.numpy as jnp
from jax import lax
from jax.experimental import pallas as pl
from jax.experimental.pallas import tpu as pltpu
from jax.sharding import PartitionSpec as P

TOPK = 8
TOP_GROUPS = 4
LANES = 128
CORES = 2
DEPTH_Z = 4
OUT_CUTS = 2
BOTH = ("outer", "inner")
BF16 = jnp.bfloat16
F32 = jnp.float32
PARAMS = pltpu.CompilerParams(vmem_limit_bytes=16 * 1024 * 1024)
IN_VMEM = pl.BlockSpec(memory_space=pltpu.VMEM)
ANYWHERE = pl.BlockSpec(memory_space=pl.ANY)


def dot(a, b):
    return jnp.dot(a, b, preferred_element_type=F32)


def dot_first(a, b):
    return lax.dot_general(a, b, (((0,), (0,)), ((), ())), preferred_element_type=F32)


def whole(shape, dtype):
    return jax.ShapeDtypeStruct(shape, dtype)


def call(kernel, out_shape, *args, **more):
    return pl.pallas_call(kernel, out_shape=out_shape, compiler_params=PARAMS, **more)(*args)


def prefetch_kernel(*refs):
    count = (len(refs) - 2) // 2
    token_ref, sem = refs[-2:]
    copies = [
        pltpu.make_async_copy(refs[at], refs[count + at], sem.at[at]) for at in range(count)
    ]
    for copy in copies:
        copy.start()
    token_ref[...] = jnp.zeros_like(token_ref)
    for copy in copies:
        copy.wait()


def far(array):
    return pltpu.with_memory_space_constraint(array, pltpu.HBM)


def near(array):
    return pltpu.with_memory_space_constraint(array, pltpu.VMEM)


def after(array, *others):
    return lax.optimization_barrier((array, *others))[0]


def prefetch(*arrays):
    arrays = [far(array) for array in arrays]
    return call(
        prefetch_kernel,
        [pltpu.VMEM(array.shape, array.dtype) for array in arrays] + [pltpu.VMEM((8, LANES), F32)],
        *arrays,
        in_specs=[ANYWHERE] * len(arrays),
        out_specs=[IN_VMEM] * (len(arrays) + 1),
        scratch_shapes=[pltpu.SemaphoreType.DMA((len(arrays),))],
    )


def prepare_kernel(tokens_ref, experts_ref, score_ref, out_ref, experts, scores, sem):
    width = tokens_ref.shape[1]
    copies = [
        pltpu.make_async_copy(experts_ref, experts, sem.at[0]),
        pltpu.make_async_copy(score_ref, scores, sem.at[1]),
        pltpu.make_async_copy(tokens_ref, out_ref.at[:, pl.ds(0, width)], sem.at[2]),
    ]
    for copy in copies:
        copy.start()
    copies[0].wait()
    copies[1].wait()
    names = jnp.concatenate([experts[...], scores[...]], axis=0).astype(F32).astype(BF16)
    slots = names.shape[0]
    row = lax.broadcasted_iota(jnp.int32, (slots, LANES), 0)
    col = lax.broadcasted_iota(jnp.int32, (slots, LANES), 1)
    spread = jnp.where(row == col, 1.0, 0.0).astype(BF16)
    out_ref[:, width:] = dot_first(names, spread).astype(BF16)
    copies[2].wait()


def prepare(tokens, experts, gate_score):
    rows, width = tokens.shape
    return call(
        prepare_kernel,
        pltpu.VMEM((rows, width + LANES), BF16),
        far(tokens),
        far(experts.T),
        far(gate_score.T),
        in_specs=[ANYWHERE] * 3,
        out_specs=IN_VMEM,
        scratch_shapes=[pltpu.VMEM((TOPK, rows), jnp.int32)] * 2 + [pltpu.SemaphoreType.DMA((3,))],
    )


def routing(meta, block_rows, capacity, group_count, expert_of):
    token_count = meta.shape[0]
    send_rows = token_count // block_rows * capacity
    total = send_rows * group_count
    slot = lax.broadcasted_iota(jnp.int32, (1, total), 1)
    group = lax.div(slot, jnp.int32(send_rows))
    expert = expert_of(group).astype(F32)
    scores = meta[:, TOPK:2 * TOPK]
    weights = 2.5 * scores / jnp.sum(scores, axis=1, keepdims=True)
    named = jnp.zeros((token_count, total), F32)
    weight = jnp.zeros((token_count, total), F32)
    for k in range(TOPK):
        match = meta[:, k:k + 1] == expert
        named = jnp.where(match, 1.0, named)
        weight = jnp.where(match, weights[:, k:k + 1], weight)
    row = lax.broadcasted_iota(jnp.int32, (token_count, token_count), 0)
    col = lax.broadcasted_iota(jnp.int32, (token_count, token_count), 1)
    rows_each = jnp.int32(block_rows)
    before = jnp.logical_and(lax.div(row, rows_each) == lax.div(col, rows_each), col < row)
    rank = dot(jnp.where(before, 1.0, 0.0).astype(BF16), named.astype(BF16))
    owner = lax.div(lax.broadcasted_iota(jnp.int32, (token_count, 1), 0), rows_each)
    wanted = (slot - group * send_rows - owner * capacity).astype(F32)
    hit = jnp.logical_and(jnp.logical_and(rank == wanted, rank < float(capacity)), named > 0.5)
    return hit, weight


def select_kernel(width, block_rows, capacity, inner_count, chips_x, blocks, *refs):
    pieces, outs = refs[:blocks], refs[blocks + 1:]
    outer_at, inner_at = lax.axis_index("outer"), lax.axis_index("inner")

    def expert_of(group):
        along_y = lax.div(group, jnp.int32(chips_x))
        along_x = group - along_y * chips_x
        return (outer_at ^ (along_x * CORES)) * inner_count + (inner_at ^ along_y)

    meta = jnp.concatenate([piece[:, width:] for piece in pieces], axis=0).astype(F32)
    hit, _ = routing(meta, block_rows, capacity, len(outs), expert_of)
    rows = jnp.concatenate([piece[:, :width] for piece in pieces], axis=0)
    chosen = dot_first(jnp.where(hit, 1.0, 0.0).astype(BF16), rows).astype(BF16)
    each = outs[0].shape[0]
    for at, out in enumerate(outs):
        out[...] = chosen[at * each:(at + 1) * each]


def hidden_kernel(width, blocks, *refs):
    pieces = refs[:blocks]
    gate_ref, up_ref, _, out_ref = refs[blocks:]
    rows = jnp.concatenate([piece[:, :width] for piece in pieces], axis=0)
    gate = dot(rows, gate_ref[...])
    up = dot(rows, up_ref[...])
    out_ref[...] = (gate / (1.0 + jnp.exp(-gate)) * up).astype(BF16)


def hidden(pieces, gate, up, loaded):
    shape = (sum(piece.shape[0] for piece in pieces), gate.shape[1])
    return call(
        functools.partial(hidden_kernel, gate.shape[0], len(pieces)),
        whole(shape, BF16),
        *pieces,
        near(gate),
        near(up),
        loaded,
        in_specs=[IN_VMEM] * (len(pieces) + 2) + [ANYWHERE],
    )


def down_kernel(start, width, chips_x, depth_y, hidden_ref, down_ref, *outs):
    answer = dot(hidden_ref[...], down_ref[:, start:start + width])
    part = outs[0].shape[0] // depth_y
    for at, out in enumerate(outs):
        along_x, core = at // CORES, at % CORES
        firsts = [((y * chips_x + along_x) * CORES + core) * part for y in range(depth_y)]
        out[...] = jnp.concatenate([answer[first:first + part] for first in firsts], axis=0).astype(BF16)


def down(rows, matrix, start, width, outer_count, depth_y):
    return call(
        functools.partial(down_kernel, start, width, outer_count // CORES, depth_y),
        [whole((rows.shape[0] // outer_count, width), BF16)] * outer_count,
        rows,
        near(matrix),
    )


def table_kernel(width, block_rows, capacity, inner_count, group_count, blocks, *refs):
    pieces, (high_ref, low_ref) = refs[:blocks], refs[blocks:]
    outer_at, inner_at = lax.axis_index("outer"), lax.axis_index("inner")
    meta = jnp.concatenate([piece[:, width:] for piece in pieces], axis=0).astype(F32)
    hit, weight = routing(
        meta, block_rows, capacity, group_count, lambda group: (outer_at ^ group) * inner_count + inner_at
    )
    weight = jnp.where(hit, weight, 0.0)
    high = weight.astype(BF16)
    high_ref[...] = high
    low_ref[...] = (weight - high.astype(F32)).astype(BF16)


def combine_kernel(blocks, start, width, hidden_ref, down_ref, high_ref, low_ref, *refs):
    answers, keep_ref, outs = refs[:blocks], refs[blocks], refs[blocks + 1:]
    rows = jnp.concatenate([answer[...] for answer in answers], axis=0)
    total = dot(hidden_ref[...], down_ref[:, start:start + width])
    total = total + dot(high_ref[...], rows) + dot(low_ref[...], rows)
    each = keep_ref.shape[0]
    keep_ref[...] = total[:each]
    for at, out in enumerate(outs):
        out[...] = total[(at + 1) * each:(at + 2) * each].astype(BF16)


def combine(shared_hidden, shared_down, high, low, answers, start, width, sends):
    each = shared_hidden.shape[0] // (sends + 1)
    return call(
        functools.partial(combine_kernel, len(answers), start, width),
        [whole((each, width), F32)] + [whole((each, width), BF16)] * sends,
        shared_hidden,
        near(shared_down),
        high,
        low,
        *answers,
    )


def add_kernel(blocks, kept_ref, *refs):
    arrived, outs = refs[:blocks], refs[blocks:]
    total = kept_ref[...]
    for block in arrived:
        total = total + block[...].astype(F32)
    each = outs[0].shape[0]
    for at, out in enumerate(outs):
        out[...] = total[at * each:(at + 1) * each].astype(out.dtype)


def finish_kernel(blocks, width, *refs):
    out_ref = refs[-1]
    for at in range((len(refs) - 1) // blocks):
        group = refs[at * blocks:(at + 1) * blocks]
        total = group[0][...]
        for block in group[1:]:
            total = total + block[...].astype(F32)
        out_ref[:, at * width:(at + 1) * width] = total.astype(BF16)


def per_device(
    tokens,
    experts,
    gate_score,
    expert_gate,
    expert_up,
    expert_down,
    shared_gate,
    shared_up,
    shared_down,
):
    rows, model_width = tokens.shape
    inner_count = lax.axis_size("inner")
    outer_count = lax.axis_size("outer")
    depth_y = inner_count // DEPTH_Z
    chips_x = outer_count // CORES
    capacity = TOPK // TOP_GROUPS * rows // inner_count
    device_count = inner_count * outer_count

    def swap(array, distance):
        return lax.ppermute(array, BOTH, [(at, at ^ distance) for at in range(device_count)])

    def along_z(k):
        return k * depth_y

    def along_outer(k):
        return k * inner_count

    sent = prepare(tokens, experts, gate_score)
    column = [sent] + [None] * (DEPTH_Z - 1)
    for k in reversed(range(1, DEPTH_Z)):
        column[k] = swap(sent, along_z(k))
    beside = [swap(sent, k) for k in range(1, depth_y)]
    other = [swap(sent, along_outer(1))]
    *expert_weights, loaded = prefetch(expert_gate[0], expert_up[0], expert_down[0])
    *beside, loaded = lax.optimization_barrier((*beside, loaded))
    for k in range(1, DEPTH_Z):
        column[k], loaded = lax.optimization_barrier((column[k], loaded))
        other.append(swap(column[k], along_outer(1)))
    at_hand = column + other

    groups = depth_y * chips_x
    blocks = call(
        functools.partial(
            select_kernel, model_width, rows, capacity, inner_count, chips_x, len(at_hand)
        ),
        [whole((CORES * DEPTH_Z * capacity, model_width), BF16)] * groups,
        *at_hand,
        loaded,
        in_specs=[IN_VMEM] * len(at_hand) + [ANYWHERE],
        out_specs=[IN_VMEM] * groups,
    )
    arrived = [blocks[0]] + [None] * (groups - 1)
    for at in reversed(range(1, groups)):
        along_y, along_x = at // chips_x, at % chips_x
        arrived[at] = swap(blocks[at], along_y + along_outer(along_x * CORES))

    segment = list(column)
    for block in beside:
        block = after(block, *blocks)
        segment.append(block)
        segment += [swap(block, along_z(k)) for k in range(1, DEPTH_Z)]
    *shared_weights, loaded = prefetch(shared_gate, shared_up, shared_down)
    *arrived, loaded = lax.optimization_barrier((*arrived, loaded))
    expert_hidden = hidden(arrived, *expert_weights[:2], loaded)
    high, low = call(
        functools.partial(
            table_kernel, model_width, rows, capacity, inner_count, outer_count, len(segment)
        ),
        [whole((rows * inner_count, device_count * capacity), BF16)] * 2,
        *segment,
        in_specs=[IN_VMEM] * len(segment),
    )
    shared_hidden = hidden(segment, *shared_weights[:2], loaded)

    out_width = model_width // OUT_CUTS
    finals = []
    for at in range(OUT_CUTS):
        start = at * out_width
        blocks = down(expert_hidden, expert_weights[2], start, out_width, outer_count, depth_y)
        answers = [blocks[0]] + [None] * (outer_count - 1)
        for k in reversed(range(1, outer_count)):
            answers[k] = swap(blocks[k], along_outer(k))
        kept, *leaving = combine(
            shared_hidden, shared_weights[2], high, low, answers, start, out_width, depth_y - 1
        )
        coming = [swap(block, k + 1) for k, block in enumerate(leaving)]
        kept, *leaving = call(
            functools.partial(add_kernel, depth_y - 1),
            [whole((rows, out_width), F32)] + [whole((rows, out_width), BF16)] * (DEPTH_Z - 1),
            kept,
            *coming,
        )
        coming = [swap(leaving[k - 1], along_z(k)) for k in reversed(range(1, DEPTH_Z))]
        finals += [kept] + coming
    return call(
        functools.partial(finish_kernel, DEPTH_Z, out_width), whole((rows, model_width), BF16), *finals
    )


def solution(mesh):
    return jax.shard_map(
        per_device,
        mesh=mesh,
        in_specs=(
            P(("outer", "inner"), None),
            P(("outer", "inner"), None),
            P(("outer", "inner"), None),
            P(("outer", "inner"), None, None),
            P(("outer", "inner"), None, None),
            P(("outer", "inner"), None, None),
            P(None, "inner"),
            P(None, "inner"),
            P("inner", None),
        ),
        out_specs=P(("outer", "inner"), None),
        check_vma=False,
    )
```

```python
import functools

import jax
import jax.numpy as jnp
from jax import lax
from jax.experimental import pallas as pl
from jax.experimental.pallas import tpu as pltpu
from jax.sharding import PartitionSpec as P

TOPK = 8
TOP_GROUPS = 4
LANES = 128
CORES = 2
DEPTH_Z = 4
OUT_CUTS = 2
BOTH = ("outer", "inner")
BF16 = jnp.bfloat16
F32 = jnp.float32
PARAMS = pltpu.CompilerParams(vmem_limit_bytes=16 * 1024 * 1024)
IN_VMEM = pl.BlockSpec(memory_space=pltpu.VMEM)
ANYWHERE = pl.BlockSpec(memory_space=pl.ANY)


def dot(a, b):
    return jnp.dot(a, b, preferred_element_type=F32)


def dot_first(a, b):
    return lax.dot_general(a, b, (((0,), (0,)), ((), ())), preferred_element_type=F32)


def whole(shape, dtype):
    return jax.ShapeDtypeStruct(shape, dtype)


def call(kernel, out_shape, *args, **more):
    return pl.pallas_call(kernel, out_shape=out_shape, compiler_params=PARAMS, **more)(*args)


def columns(ref, at, width):
    return ref if ref.shape[1] == width else ref.at[:, pl.ds(at * width, width)]


def prefetch_kernel(cuts, *refs):
    token_ref, sem = refs[-2:]
    count = len(cuts)
    outs = refs[-2 - count:-2]
    copies = [
        pltpu.make_async_copy(columns(refs[at], cut, outs[at].shape[1]), outs[at], sem.at[at])
        for at, cut in enumerate(cuts)
    ]
    for copy in copies:
        copy.start()
    token_ref[...] = jnp.zeros_like(token_ref)
    for copy in copies:
        copy.wait()


def far(array):
    return pltpu.with_memory_space_constraint(array, pltpu.HBM)


def near(array):
    return pltpu.with_memory_space_constraint(array, pltpu.VMEM)


def after(array, *others):
    return lax.optimization_barrier((array, *others))[0]


def prefetch(*arrays, half=None, order=None):
    shapes = [array.shape for array in arrays]
    if half is not None:
        arrays += (half,)
        shapes.append((half.shape[0], half.shape[1] // OUT_CUTS))
    arrays = [far(array) for array in arrays]
    orders = [] if order is None else [order]
    return call(
        functools.partial(prefetch_kernel, [0] * len(arrays)),
        [pltpu.VMEM(shape, BF16) for shape in shapes] + [pltpu.VMEM((8, LANES), F32)],
        *arrays,
        *orders,
        in_specs=[ANYWHERE] * (len(arrays) + len(orders)),
        out_specs=[IN_VMEM] * (len(arrays) + 1),
        scratch_shapes=[pltpu.SemaphoreType.DMA((len(arrays),))],
    )


def prepare_kernel(tokens_ref, experts_ref, score_ref, out_ref, experts, scores, sem):
    width = tokens_ref.shape[1]
    copies = [
        pltpu.make_async_copy(experts_ref, experts, sem.at[0]),
        pltpu.make_async_copy(score_ref, scores, sem.at[1]),
        pltpu.make_async_copy(tokens_ref, out_ref.at[:, pl.ds(0, width)], sem.at[2]),
    ]
    for copy in copies:
        copy.start()
    copies[0].wait()
    copies[1].wait()
    names = jnp.concatenate([experts[...], scores[...]], axis=0).astype(F32).astype(BF16)
    slots = names.shape[0]
    row = lax.broadcasted_iota(jnp.int32, (slots, LANES), 0)
    col = lax.broadcasted_iota(jnp.int32, (slots, LANES), 1)
    spread = jnp.where(row == col, 1.0, 0.0).astype(BF16)
    out_ref[:, width:] = dot_first(names, spread).astype(BF16)
    copies[2].wait()


def prepare(tokens, experts, gate_score):
    rows, width = tokens.shape
    return call(
        prepare_kernel,
        pltpu.VMEM((rows, width + LANES), BF16),
        far(tokens),
        far(experts.T),
        far(gate_score.T),
        in_specs=[ANYWHERE] * 3,
        out_specs=IN_VMEM,
        scratch_shapes=[pltpu.VMEM((TOPK, rows), jnp.int32)] * 2 + [pltpu.SemaphoreType.DMA((3,))],
    )


def routing(meta, block_rows, capacity, group_count, expert_of):
    token_count = meta.shape[0]
    send_rows = token_count // block_rows * capacity
    total = send_rows * group_count
    slot = lax.broadcasted_iota(jnp.int32, (1, total), 1)
    group = lax.div(slot, jnp.int32(send_rows))
    expert = expert_of(group).astype(F32)
    scores = meta[:, TOPK:2 * TOPK]
    weights = 2.5 * scores / jnp.sum(scores, axis=1, keepdims=True)
    named = jnp.zeros((token_count, total), F32)
    weight = jnp.zeros((token_count, total), F32)
    for k in range(TOPK):
        match = meta[:, k:k + 1] == expert
        named = jnp.where(match, 1.0, named)
        weight = jnp.where(match, weights[:, k:k + 1], weight)
    row = lax.broadcasted_iota(jnp.int32, (token_count, token_count), 0)
    col = lax.broadcasted_iota(jnp.int32, (token_count, token_count), 1)
    rows_each = jnp.int32(block_rows)
    before = jnp.logical_and(lax.div(row, rows_each) == lax.div(col, rows_each), col < row)
    rank = dot(jnp.where(before, 1.0, 0.0).astype(BF16), named.astype(BF16))
    owner = lax.div(lax.broadcasted_iota(jnp.int32, (token_count, 1), 0), rows_each)
    wanted = (slot - group * send_rows - owner * capacity).astype(F32)
    hit = jnp.logical_and(jnp.logical_and(rank == wanted, rank < float(capacity)), named > 0.5)
    return hit, weight


def select_kernel(width, block_rows, capacity, inner_count, chips_x, blocks, *refs):
    pieces, outs = refs[:blocks], refs[blocks + 1:]
    outer_at, inner_at = lax.axis_index("outer"), lax.axis_index("inner")

    def expert_of(group):
        along_y = lax.div(group, jnp.int32(chips_x))
        along_x = group - along_y * chips_x
        return (outer_at ^ (along_x * CORES)) * inner_count + (inner_at ^ along_y)

    meta = jnp.concatenate([piece[:, width:] for piece in pieces], axis=0).astype(F32)
    hit, _ = routing(meta, block_rows, capacity, len(outs), expert_of)
    rows = jnp.concatenate([piece[:, :width] for piece in pieces], axis=0)
    chosen = dot_first(jnp.where(hit, 1.0, 0.0).astype(BF16), rows).astype(BF16)
    each = outs[0].shape[0]
    for at, out in enumerate(outs):
        out[...] = chosen[at * each:(at + 1) * each]


def hidden_kernel(width, blocks, *refs):
    pieces, (gate_ref, up_ref, _), refs = refs[:blocks], refs[blocks:blocks + 3], refs[blocks + 3:]
    copies = []
    if len(refs) > 1:
        source, refs, sem = refs[0], refs[1:-1], refs[-1]
        copies = [
            pltpu.make_async_copy(columns(source, at, target.shape[1]), target, sem.at[at - 1])
            for at, target in enumerate(refs[1:], 1)
        ]
    for copy in copies:
        copy.start()
    rows = jnp.concatenate([piece[:, :width] for piece in pieces], axis=0)
    gate = dot(rows, gate_ref[...])
    up = dot(rows, up_ref[...])
    refs[0][...] = (gate / (1.0 + jnp.exp(-gate)) * up).astype(BF16)
    for copy in copies:
        copy.wait()


def hidden(pieces, gate, up, loaded, *later):
    shapes = [(sum(piece.shape[0] for piece in pieces), gate.shape[1])]
    for array in later:
        shapes += [(array.shape[0], array.shape[1] // OUT_CUTS)] * (OUT_CUTS - 1)
    return call(
        functools.partial(hidden_kernel, gate.shape[0], len(pieces)),
        [pltpu.VMEM(shape, BF16) for shape in shapes],
        *pieces,
        near(gate),
        near(up),
        loaded,
        *[far(array) for array in later],
        in_specs=[IN_VMEM] * (len(pieces) + 2) + [ANYWHERE] * (1 + len(later)),
        out_specs=[IN_VMEM] * len(shapes),
        scratch_shapes=[pltpu.SemaphoreType.DMA((OUT_CUTS - 1,))] if later else [],
    )


def down_kernel(chips_x, depth_y, hidden_ref, down_ref, *outs):
    answer = dot(hidden_ref[...], down_ref[...])
    part = outs[0].shape[0] // depth_y
    for at, out in enumerate(outs):
        along_x, core = at // CORES, at % CORES
        firsts = [((y * chips_x + along_x) * CORES + core) * part for y in range(depth_y)]
        out[...] = jnp.concatenate([answer[first:first + part] for first in firsts], axis=0).astype(BF16)


def down(rows, matrix, outer_count, depth_y):
    return call(
        functools.partial(down_kernel, outer_count // CORES, depth_y),
        [whole((rows.shape[0] // outer_count, matrix.shape[1]), BF16)] * outer_count,
        rows,
        near(matrix),
    )


def table_kernel(width, block_rows, capacity, inner_count, group_count, blocks, *refs):
    pieces, (high_ref, low_ref) = refs[:blocks], refs[blocks:]
    outer_at, inner_at = lax.axis_index("outer"), lax.axis_index("inner")
    meta = jnp.concatenate([piece[:, width:] for piece in pieces], axis=0).astype(F32)
    hit, weight = routing(
        meta, block_rows, capacity, group_count, lambda group: (outer_at ^ group) * inner_count + inner_at
    )
    weight = jnp.where(hit, weight, 0.0)
    high = weight.astype(BF16)
    high_ref[...] = high
    low_ref[...] = (weight - high.astype(F32)).astype(BF16)


def combine_kernel(blocks, start, width, hidden_ref, down_ref, high_ref, low_ref, *refs):
    answers, keep_ref, outs = refs[:blocks], refs[blocks], refs[blocks + 1:]
    rows = jnp.concatenate([answer[...] for answer in answers], axis=0)
    total = dot(hidden_ref[...], down_ref[:, start:start + width])
    total = total + dot(high_ref[...], rows) + dot(low_ref[...], rows)
    each = keep_ref.shape[0]
    keep_ref[...] = total[:each]
    for at, out in enumerate(outs):
        out[...] = total[(at + 1) * each:(at + 2) * each].astype(BF16)


def combine(shared_hidden, shared_down, high, low, answers, start, width, sends):
    each = shared_hidden.shape[0] // (sends + 1)
    return call(
        functools.partial(combine_kernel, len(answers), start, width),
        [whole((each, width), F32)] + [whole((each, width), BF16)] * sends,
        shared_hidden,
        near(shared_down),
        high,
        low,
        *answers,
    )


def add_kernel(blocks, kept_ref, *refs):
    arrived, outs = refs[:blocks], refs[blocks:]
    total = kept_ref[...]
    for block in arrived:
        total = total + block[...].astype(F32)
    each = outs[0].shape[0]
    for at, out in enumerate(outs):
        out[...] = total[at * each:(at + 1) * each].astype(out.dtype)


def finish_kernel(blocks, width, *refs):
    out_ref = refs[-1]
    for at in range((len(refs) - 1) // blocks):
        group = refs[at * blocks:(at + 1) * blocks]
        total = group[0][...]
        for block in group[1:]:
            total = total + block[...].astype(F32)
        out_ref[:, at * width:(at + 1) * width] = total.astype(BF16)


def per_device(
    tokens,
    experts,
    gate_score,
    expert_gate,
    expert_up,
    expert_down,
    shared_gate,
    shared_up,
    shared_down,
):
    rows, model_width = tokens.shape
    inner_count = lax.axis_size("inner")
    outer_count = lax.axis_size("outer")
    depth_y = inner_count // DEPTH_Z
    chips_x = outer_count // CORES
    capacity = TOPK // TOP_GROUPS * rows // inner_count
    device_count = inner_count * outer_count

    def swap(array, distance):
        return lax.ppermute(array, BOTH, [(at, at ^ distance) for at in range(device_count)])

    def along_z(k):
        return k * depth_y

    def along_outer(k):
        return k * inner_count

    sent = prepare(tokens, experts, gate_score)
    column = [sent] + [None] * (DEPTH_Z - 1)
    for k in reversed(range(1, DEPTH_Z)):
        column[k] = swap(sent, along_z(k))
    beside = [swap(sent, k) for k in range(1, depth_y)]
    gate, up, first_down, loaded = prefetch(
        expert_gate[0], expert_up[0], half=expert_down[0], order=sent
    )
    column[DEPTH_Z - 1], loaded = lax.optimization_barrier((column[DEPTH_Z - 1], loaded))
    *beside, loaded = lax.optimization_barrier((*beside, loaded))
    other = [None] * DEPTH_Z
    for k in reversed(range(DEPTH_Z)):
        other[k] = swap(column[k], along_outer(1))
    at_hand = column + other

    groups = depth_y * chips_x
    blocks = call(
        functools.partial(
            select_kernel, model_width, rows, capacity, inner_count, chips_x, len(at_hand)
        ),
        [whole((CORES * DEPTH_Z * capacity, model_width), BF16)] * groups,
        *at_hand,
        loaded,
        in_specs=[IN_VMEM] * len(at_hand) + [ANYWHERE],
        out_specs=[IN_VMEM] * groups,
    )
    arrived = [blocks[0]] + [None] * (groups - 1)
    for at in reversed(range(1, groups)):
        along_y, along_x = at // chips_x, at % chips_x
        arrived[at] = swap(blocks[at], along_y + along_outer(along_x * CORES))

    segment = list(column)
    for block in beside:
        block = after(block, *blocks)
        segment.append(block)
        segment += [swap(block, along_z(k)) for k in range(1, DEPTH_Z)]
    *shared_weights, loaded = prefetch(shared_gate, shared_up, shared_down)
    *arrived, loaded = lax.optimization_barrier((*arrived, loaded))
    expert_hidden, *down_weights = hidden(arrived, gate, up, loaded, expert_down[0])
    down_weights = [first_down] + down_weights
    high, low = call(
        functools.partial(
            table_kernel, model_width, rows, capacity, inner_count, outer_count, len(segment)
        ),
        [whole((rows * inner_count, device_count * capacity), BF16)] * 2,
        *segment,
        in_specs=[IN_VMEM] * len(segment),
    )
    (shared_hidden,) = hidden(segment, *shared_weights[:2], loaded)

    out_width = model_width // OUT_CUTS
    finals = []
    for at in range(OUT_CUTS):
        start = at * out_width
        blocks = down(expert_hidden, down_weights[at], outer_count, depth_y)
        answers = [blocks[0]] + [None] * (outer_count - 1)
        for k in reversed(range(1, outer_count)):
            answers[k] = swap(blocks[k], along_outer(k))
        kept, *leaving = combine(
            shared_hidden, shared_weights[2], high, low, answers, start, out_width, depth_y - 1
        )
        coming = [swap(block, k + 1) for k, block in enumerate(leaving)]
        kept, *leaving = call(
            functools.partial(add_kernel, depth_y - 1),
            [whole((rows, out_width), F32)] + [whole((rows, out_width), BF16)] * (DEPTH_Z - 1),
            kept,
            *coming,
        )
        coming = [swap(leaving[k - 1], along_z(k)) for k in reversed(range(1, DEPTH_Z))]
        finals += [kept] + coming
    return call(
        functools.partial(finish_kernel, DEPTH_Z, out_width), whole((rows, model_width), BF16), *finals
    )


def solution(mesh):
    return jax.shard_map(
        per_device,
        mesh=mesh,
        in_specs=(
            P(("outer", "inner"), None),
            P(("outer", "inner"), None),
            P(("outer", "inner"), None),
            P(("outer", "inner"), None, None),
            P(("outer", "inner"), None, None),
            P(("outer", "inner"), None, None),
            P(None, "inner"),
            P(None, "inner"),
            P("inner", None),
        ),
        out_specs=P(("outer", "inner"), None),
        check_vma=False,
    )
```

```python
import functools

import jax
import jax.numpy as jnp
from jax import lax
from jax.experimental import pallas as pl
from jax.experimental.pallas import tpu as pltpu
from jax.sharding import PartitionSpec as P

TOPK = 8
TOP_GROUPS = 4
LANES = 128
CORES = 2
DEPTH_Z = 4
FIRST_Z = 2
WAY_BACK = (3, 2, 1)
WAY_SHARED = (2, 1, 3)
OUT_CUTS = 2
BOTH = ("outer", "inner")
BF16 = jnp.bfloat16
F32 = jnp.float32
PARAMS = pltpu.CompilerParams(vmem_limit_bytes=16 * 1024 * 1024)
IN_VMEM = pl.BlockSpec(memory_space=pltpu.VMEM)
ANYWHERE = pl.BlockSpec(memory_space=pl.ANY)


def dot(a, b):
    return jnp.dot(a, b, preferred_element_type=F32)


def dot_first(a, b):
    return lax.dot_general(a, b, (((0,), (0,)), ((), ())), preferred_element_type=F32)


def whole(shape, dtype):
    return jax.ShapeDtypeStruct(shape, dtype)


def call(kernel, out_shape, *args, **more):
    return pl.pallas_call(kernel, out_shape=out_shape, compiler_params=PARAMS, **more)(*args)


def columns(ref, at, width):
    return ref if ref.shape[1] == width else ref.at[:, pl.ds(at * width, width)]


def prefetch_kernel(cuts, *refs):
    token_ref, sem = refs[-2:]
    count = len(cuts)
    outs = refs[-2 - count:-2]
    copies = [
        pltpu.make_async_copy(columns(refs[at], cut, outs[at].shape[1]), outs[at], sem.at[at])
        for at, cut in enumerate(cuts)
    ]
    for copy in copies:
        copy.start()
    token_ref[...] = jnp.zeros_like(token_ref)
    for copy in copies:
        copy.wait()


def far(array):
    return pltpu.with_memory_space_constraint(array, pltpu.HBM)


def near(array):
    return pltpu.with_memory_space_constraint(array, pltpu.VMEM)


def after(array, *others):
    return lax.optimization_barrier((array, *others))[0]


def prefetch(*arrays, half=None, order=None):
    shapes = [array.shape for array in arrays]
    if half is not None:
        arrays += (half,)
        shapes.append((half.shape[0], half.shape[1] // OUT_CUTS))
    arrays = [far(array) for array in arrays]
    orders = [] if order is None else [order]
    return call(
        functools.partial(prefetch_kernel, [0] * len(arrays)),
        [pltpu.VMEM(shape, BF16) for shape in shapes] + [pltpu.VMEM((8, LANES), F32)],
        *arrays,
        *orders,
        in_specs=[ANYWHERE] * (len(arrays) + len(orders)),
        out_specs=[IN_VMEM] * (len(arrays) + 1),
        scratch_shapes=[pltpu.SemaphoreType.DMA((len(arrays),))],
    )


def prepare_kernel(tokens_ref, experts_ref, score_ref, out_ref, experts, scores, sem):
    width = tokens_ref.shape[1]
    copies = [
        pltpu.make_async_copy(experts_ref, experts, sem.at[0]),
        pltpu.make_async_copy(score_ref, scores, sem.at[1]),
        pltpu.make_async_copy(tokens_ref, out_ref.at[:, pl.ds(0, width)], sem.at[2]),
    ]
    for copy in copies:
        copy.start()
    copies[0].wait()
    copies[1].wait()
    names = jnp.concatenate([experts[...], scores[...]], axis=0).astype(F32).astype(BF16)
    slots = names.shape[0]
    row = lax.broadcasted_iota(jnp.int32, (slots, LANES), 0)
    col = lax.broadcasted_iota(jnp.int32, (slots, LANES), 1)
    spread = jnp.where(row == col, 1.0, 0.0).astype(BF16)
    out_ref[:, width:] = dot_first(names, spread).astype(BF16)
    copies[2].wait()


def prepare(tokens, experts, gate_score):
    rows, width = tokens.shape
    return call(
        prepare_kernel,
        pltpu.VMEM((rows, width + LANES), BF16),
        far(tokens),
        far(experts.T),
        far(gate_score.T),
        in_specs=[ANYWHERE] * 3,
        out_specs=IN_VMEM,
        scratch_shapes=[pltpu.VMEM((TOPK, rows), jnp.int32)] * 2 + [pltpu.SemaphoreType.DMA((3,))],
    )


def routing(meta, block_rows, capacity, group_count, expert_of):
    token_count = meta.shape[0]
    send_rows = token_count // block_rows * capacity
    total = send_rows * group_count
    slot = lax.broadcasted_iota(jnp.int32, (1, total), 1)
    group = lax.div(slot, jnp.int32(send_rows))
    expert = expert_of(group).astype(F32)
    scores = meta[:, TOPK:2 * TOPK]
    weights = 2.5 * scores / jnp.sum(scores, axis=1, keepdims=True)
    named = jnp.zeros((token_count, total), F32)
    weight = jnp.zeros((token_count, total), F32)
    for k in range(TOPK):
        match = meta[:, k:k + 1] == expert
        named = jnp.where(match, 1.0, named)
        weight = jnp.where(match, weights[:, k:k + 1], weight)
    row = lax.broadcasted_iota(jnp.int32, (token_count, token_count), 0)
    col = lax.broadcasted_iota(jnp.int32, (token_count, token_count), 1)
    rows_each = jnp.int32(block_rows)
    before = jnp.logical_and(lax.div(row, rows_each) == lax.div(col, rows_each), col < row)
    rank = dot(jnp.where(before, 1.0, 0.0).astype(BF16), named.astype(BF16))
    owner = lax.div(lax.broadcasted_iota(jnp.int32, (token_count, 1), 0), rows_each)
    wanted = (slot - group * send_rows - owner * capacity).astype(F32)
    hit = jnp.logical_and(jnp.logical_and(rank == wanted, rank < float(capacity)), named > 0.5)
    return hit, weight


def select_kernel(width, block_rows, capacity, inner_count, chips_x, blocks, *refs):
    pieces, outs = refs[:blocks], refs[blocks + 1:]
    outer_at, inner_at = lax.axis_index("outer"), lax.axis_index("inner")

    def expert_of(group):
        along_y = lax.div(group, jnp.int32(chips_x))
        along_x = group - along_y * chips_x
        return (outer_at ^ (along_x * CORES)) * inner_count + (inner_at ^ along_y)

    meta = jnp.concatenate([piece[:, width:] for piece in pieces], axis=0).astype(F32)
    hit, _ = routing(meta, block_rows, capacity, len(outs), expert_of)
    rows = jnp.concatenate([piece[:, :width] for piece in pieces], axis=0)
    chosen = dot_first(jnp.where(hit, 1.0, 0.0).astype(BF16), rows).astype(BF16)
    each = outs[0].shape[0]
    for at, out in enumerate(outs):
        out[...] = chosen[at * each:(at + 1) * each]


def hidden_kernel(width, blocks, *refs):
    pieces, (gate_ref, up_ref, _), refs = refs[:blocks], refs[blocks:blocks + 3], refs[blocks + 3:]
    copies = []
    if len(refs) > 1:
        source, refs, sem = refs[0], refs[1:-1], refs[-1]
        copies = [
            pltpu.make_async_copy(columns(source, at, target.shape[1]), target, sem.at[at - 1])
            for at, target in enumerate(refs[1:], 1)
        ]
    for copy in copies:
        copy.start()
    rows = jnp.concatenate([piece[:, :width] for piece in pieces], axis=0)
    gate = dot(rows, gate_ref[...])
    up = dot(rows, up_ref[...])
    refs[0][...] = (gate / (1.0 + jnp.exp(-gate)) * up).astype(BF16)
    for copy in copies:
        copy.wait()


def hidden(pieces, gate, up, loaded, *later):
    shapes = [(sum(piece.shape[0] for piece in pieces), gate.shape[1])]
    for array in later:
        shapes += [(array.shape[0], array.shape[1] // OUT_CUTS)] * (OUT_CUTS - 1)
    return call(
        functools.partial(hidden_kernel, gate.shape[0], len(pieces)),
        [pltpu.VMEM(shape, BF16) for shape in shapes],
        *pieces,
        near(gate),
        near(up),
        loaded,
        *[far(array) for array in later],
        in_specs=[IN_VMEM] * (len(pieces) + 2) + [ANYWHERE] * (1 + len(later)),
        out_specs=[IN_VMEM] * len(shapes),
        scratch_shapes=[pltpu.SemaphoreType.DMA((OUT_CUTS - 1,))] if later else [],
    )


def down_kernel(chips_x, depth_y, hidden_ref, down_ref, *outs):
    answer = dot(hidden_ref[...], down_ref[...])
    part = outs[0].shape[0] // depth_y
    for at, out in enumerate(outs):
        along_x, core = at // CORES, at % CORES
        firsts = [((y * chips_x + along_x) * CORES + core) * part for y in range(depth_y)]
        out[...] = jnp.concatenate([answer[first:first + part] for first in firsts], axis=0).astype(BF16)


def down(rows, matrix, outer_count, depth_y):
    return call(
        functools.partial(down_kernel, outer_count // CORES, depth_y),
        [whole((rows.shape[0] // outer_count, matrix.shape[1]), BF16)] * outer_count,
        rows,
        near(matrix),
    )


def table_kernel(width, block_rows, capacity, inner_count, group_count, blocks, *refs):
    pieces, (high_ref, low_ref) = refs[:blocks], refs[blocks:]
    outer_at, inner_at = lax.axis_index("outer"), lax.axis_index("inner")
    meta = jnp.concatenate([piece[:, width:] for piece in pieces], axis=0).astype(F32)
    hit, weight = routing(
        meta, block_rows, capacity, group_count, lambda group: (outer_at ^ group) * inner_count + inner_at
    )
    weight = jnp.where(hit, weight, 0.0)
    high = weight.astype(BF16)
    high_ref[...] = high
    low_ref[...] = (weight - high.astype(F32)).astype(BF16)


def shared_kernel(hidden_ref, down_ref, *outs):
    width = outs[0].shape[1]
    for at, out in enumerate(outs):
        out[...] = dot(hidden_ref[...], down_ref[:, at * width:(at + 1) * width])


def combine_kernel(blocks, base_ref, high_ref, low_ref, *refs):
    answers, keep_ref, outs = refs[:blocks], refs[blocks], refs[blocks + 1:]
    answers = [answers[0], answers[-1], *answers[1:-1]]
    rows = jnp.concatenate([answer[...] for answer in answers], axis=0)
    total = base_ref[...] + dot(high_ref[...], rows) + dot(low_ref[...], rows)
    each = keep_ref.shape[0]
    keep_ref[...] = total[:each]
    for at, out in enumerate(outs):
        out[...] = total[(at + 1) * each:(at + 2) * each].astype(BF16)


def combine(base, high, low, answers, sends):
    each, width = base.shape[0] // (sends + 1), base.shape[1]
    return call(
        functools.partial(combine_kernel, len(answers)),
        [whole((each, width), F32)] + [whole((each, width), BF16)] * sends,
        base,
        high,
        low,
        answers[0],
        *answers[2:],
        answers[1],
    )


def add_kernel(blocks, kept_ref, *refs):
    arrived, outs = refs[:blocks], refs[blocks:]
    total = kept_ref[...]
    for block in arrived:
        total = total + block[...].astype(F32)
    each = outs[0].shape[0]
    for at, out in enumerate(outs):
        out[...] = total[at * each:(at + 1) * each].astype(out.dtype)


def finish_kernel(blocks, width, *refs):
    out_ref = refs[-1]
    for at in range((len(refs) - 1) // blocks):
        group = refs[at * blocks:(at + 1) * blocks]
        total = group[0][...]
        for block in group[1:]:
            total = total + block[...].astype(F32)
        out_ref[:, at * width:(at + 1) * width] = total.astype(BF16)


def per_device(
    tokens,
    experts,
    gate_score,
    expert_gate,
    expert_up,
    expert_down,
    shared_gate,
    shared_up,
    shared_down,
):
    rows, model_width = tokens.shape
    inner_count = lax.axis_size("inner")
    outer_count = lax.axis_size("outer")
    depth_y = inner_count // DEPTH_Z
    chips_x = outer_count // CORES
    capacity = TOPK // TOP_GROUPS * rows // inner_count
    device_count = inner_count * outer_count

    def swap(array, distance):
        return lax.ppermute(array, BOTH, [(at, at ^ distance) for at in range(device_count)])

    def along_z(k):
        return k * depth_y

    def along_outer(k):
        return k * inner_count

    sent = prepare(tokens, experts, gate_score)
    column = [sent] + [None] * (DEPTH_Z - 1)
    for k in reversed(range(1, DEPTH_Z)):
        column[k] = swap(sent, along_z(k))
    beside = [swap(sent, k) for k in range(1, depth_y)]
    gate, up, loaded = prefetch(expert_gate[0], expert_up[0], order=sent)
    column[FIRST_Z], loaded = lax.optimization_barrier((column[FIRST_Z], loaded))
    *beside, loaded = lax.optimization_barrier((*beside, loaded))
    other = [None] * DEPTH_Z
    for k in reversed(range(DEPTH_Z)):
        other[k] = swap(column[k], along_outer(1))
    at_hand = column + other

    groups = depth_y * chips_x
    blocks = call(
        functools.partial(
            select_kernel, model_width, rows, capacity, inner_count, chips_x, len(at_hand)
        ),
        [whole((CORES * DEPTH_Z * capacity, model_width), BF16)] * groups,
        *at_hand,
        loaded,
        in_specs=[IN_VMEM] * len(at_hand) + [ANYWHERE],
        out_specs=[IN_VMEM] * groups,
    )
    arrived = [blocks[0]] + [None] * (groups - 1)
    for at in reversed(range(1, groups)):
        along_y, along_x = at // chips_x, at % chips_x
        arrived[at] = swap(blocks[at], along_y + along_outer(along_x * CORES))

    segment = list(column)
    for block in beside:
        block = after(block, *blocks)
        segment.append(block)
        moved = {k: swap(block, along_z(k)) for k in WAY_SHARED}
        for k, block in zip(WAY_SHARED, lax.optimization_barrier(tuple(moved.values()))):
            moved[k] = block
        segment += [moved[k] for k in range(1, DEPTH_Z)]
    *shared_weights, first_down, loaded = prefetch(
        shared_gate, shared_up, shared_down, half=expert_down[0]
    )
    way = sorted(range(groups), key=lambda at: (at % chips_x > 0, at // chips_x > 0, at))
    *coming, loaded = lax.optimization_barrier((*[arrived[at] for at in way], loaded))
    for at, block in zip(way, coming):
        arrived[at] = block
    expert_hidden, *down_weights = hidden(arrived, gate, up, loaded, expert_down[0])
    down_weights = [first_down] + down_weights
    high, low = call(
        functools.partial(
            table_kernel, model_width, rows, capacity, inner_count, outer_count, len(segment)
        ),
        [whole((rows * inner_count, device_count * capacity), BF16)] * 2,
        *segment,
        in_specs=[IN_VMEM] * len(segment),
    )
    (shared_hidden,) = hidden(segment, *shared_weights[:2], loaded)

    bases = call(
        shared_kernel,
        [whole((rows * inner_count, model_width // OUT_CUTS), F32)] * OUT_CUTS,
        shared_hidden,
        near(shared_weights[2]),
    )

    out_width = model_width // OUT_CUTS
    finals = []
    for at in range(OUT_CUTS):
        blocks = down(expert_hidden, down_weights[at], outer_count, depth_y)
        answers = [blocks[0]] + [None] * (outer_count - 1)
        for k in reversed(range(1, outer_count)):
            answers[k] = swap(blocks[k], along_outer(k))
        kept, *leaving = combine(bases[at], high, low, answers, depth_y - 1)
        coming = [swap(block, k + 1) for k, block in enumerate(leaving)]
        kept, *leaving = call(
            functools.partial(add_kernel, depth_y - 1),
            [whole((rows, out_width), F32)] + [whole((rows, out_width), BF16)] * (DEPTH_Z - 1),
            kept,
            *coming,
        )
        coming = [swap(leaving[k - 1], along_z(k)) for k in WAY_BACK]
        finals += [kept] + coming
    return call(
        functools.partial(finish_kernel, DEPTH_Z, out_width), whole((rows, model_width), BF16), *finals
    )


def solution(mesh):
    return jax.shard_map(
        per_device,
        mesh=mesh,
        in_specs=(
            P(("outer", "inner"), None),
            P(("outer", "inner"), None),
            P(("outer", "inner"), None),
            P(("outer", "inner"), None, None),
            P(("outer", "inner"), None, None),
            P(("outer", "inner"), None, None),
            P(None, "inner"),
            P(None, "inner"),
            P("inner", None),
        ),
        out_specs=P(("outer", "inner"), None),
        check_vma=False,
    )
```

```python
import functools

import jax
import jax.numpy as jnp
from jax import lax
from jax.experimental import pallas as pl
from jax.experimental.pallas import tpu as pltpu
from jax.sharding import PartitionSpec as P

TOPK = 8
TOP_GROUPS = 4
LANES = 128
CORES = 2
DEPTH_Z = 4
FIRST_Z = 2
WAY_BACK = (3, 2, 1)
WAY_SHARED = (2, 1, 3)
OUT_CUTS = 2
BOTH = ("outer", "inner")
BF16 = jnp.bfloat16
F32 = jnp.float32
PARAMS = pltpu.CompilerParams(vmem_limit_bytes=16 * 1024 * 1024)
IN_VMEM = pl.BlockSpec(memory_space=pltpu.VMEM)
ANYWHERE = pl.BlockSpec(memory_space=pl.ANY)


def dot(a, b):
    return jnp.dot(a, b, preferred_element_type=F32)


def dot_first(a, b):
    return lax.dot_general(a, b, (((0,), (0,)), ((), ())), preferred_element_type=F32)


def whole(shape, dtype):
    return jax.ShapeDtypeStruct(shape, dtype)


def call(kernel, out_shape, *args, **more):
    return pl.pallas_call(kernel, out_shape=out_shape, compiler_params=PARAMS, **more)(*args)


def columns(ref, at, width):
    return ref if ref.shape[1] == width else ref.at[:, pl.ds(at * width, width)]


def prefetch_kernel(cuts, *refs):
    token_ref, sem = refs[-2:]
    count = len(cuts)
    outs = refs[-2 - count:-2]
    copies = [
        pltpu.make_async_copy(columns(refs[at], cut, outs[at].shape[1]), outs[at], sem.at[at])
        for at, cut in enumerate(cuts)
    ]
    for copy in copies:
        copy.start()
    token_ref[...] = jnp.zeros_like(token_ref)
    for copy in copies:
        copy.wait()


def far(array):
    return pltpu.with_memory_space_constraint(array, pltpu.HBM)


def near(array):
    return pltpu.with_memory_space_constraint(array, pltpu.VMEM)


def after(array, *others):
    return lax.optimization_barrier((array, *others))[0]


def prefetch(*arrays, half=None, order=None):
    shapes = [array.shape for array in arrays]
    if half is not None:
        arrays += (half,)
        shapes.append((half.shape[0], half.shape[1] // OUT_CUTS))
    arrays = [far(array) for array in arrays]
    orders = [] if order is None else [order]
    return call(
        functools.partial(prefetch_kernel, [0] * len(arrays)),
        [pltpu.VMEM(shape, BF16) for shape in shapes] + [pltpu.VMEM((8, LANES), F32)],
        *arrays,
        *orders,
        in_specs=[ANYWHERE] * (len(arrays) + len(orders)),
        out_specs=[IN_VMEM] * (len(arrays) + 1),
        scratch_shapes=[pltpu.SemaphoreType.DMA((len(arrays),))],
    )


def prepare_kernel(tokens_ref, experts_ref, score_ref, out_ref, experts, scores, sem):
    width = tokens_ref.shape[1]
    copies = [
        pltpu.make_async_copy(experts_ref, experts, sem.at[0]),
        pltpu.make_async_copy(score_ref, scores, sem.at[1]),
        pltpu.make_async_copy(tokens_ref, out_ref.at[:, pl.ds(0, width)], sem.at[2]),
    ]
    for copy in copies:
        copy.start()
    copies[0].wait()
    copies[1].wait()
    names = jnp.concatenate([experts[...], scores[...]], axis=0).astype(F32).astype(BF16)
    slots = names.shape[0]
    row = lax.broadcasted_iota(jnp.int32, (slots, LANES), 0)
    col = lax.broadcasted_iota(jnp.int32, (slots, LANES), 1)
    spread = jnp.where(row == col, 1.0, 0.0).astype(BF16)
    out_ref[:, width:] = dot_first(names, spread).astype(BF16)
    copies[2].wait()


def prepare(tokens, experts, gate_score):
    rows, width = tokens.shape
    return call(
        prepare_kernel,
        pltpu.VMEM((rows, width + LANES), BF16),
        far(tokens),
        far(experts.T),
        far(gate_score.T),
        in_specs=[ANYWHERE] * 3,
        out_specs=IN_VMEM,
        scratch_shapes=[pltpu.VMEM((TOPK, rows), jnp.int32)] * 2 + [pltpu.SemaphoreType.DMA((3,))],
    )


def routing(meta, block_rows, capacity, group_count, expert_of):
    token_count = meta.shape[0]
    send_rows = token_count // block_rows * capacity
    total = send_rows * group_count
    slot = lax.broadcasted_iota(jnp.int32, (1, total), 1)
    group = lax.div(slot, jnp.int32(send_rows))
    expert = expert_of(group).astype(F32)
    scores = meta[:, TOPK:2 * TOPK]
    weights = 2.5 * scores / jnp.sum(scores, axis=1, keepdims=True)
    named = jnp.zeros((token_count, total), F32)
    weight = jnp.zeros((token_count, total), F32)
    for k in range(TOPK):
        match = meta[:, k:k + 1] == expert
        named = jnp.where(match, 1.0, named)
        weight = jnp.where(match, weights[:, k:k + 1], weight)
    row = lax.broadcasted_iota(jnp.int32, (token_count, token_count), 0)
    col = lax.broadcasted_iota(jnp.int32, (token_count, token_count), 1)
    rows_each = jnp.int32(block_rows)
    before = jnp.logical_and(lax.div(row, rows_each) == lax.div(col, rows_each), col < row)
    rank = dot(jnp.where(before, 1.0, 0.0).astype(BF16), named.astype(BF16))
    owner = lax.div(lax.broadcasted_iota(jnp.int32, (token_count, 1), 0), rows_each)
    wanted = (slot - group * send_rows - owner * capacity).astype(F32)
    hit = jnp.logical_and(jnp.logical_and(rank == wanted, rank < float(capacity)), named > 0.5)
    return hit, weight


def chosen_rows(width, block_rows, capacity, inner_count, chips_x, groups, pieces):
    outer_at, inner_at = lax.axis_index("outer"), lax.axis_index("inner")

    def expert_of(group):
        along_y = lax.div(group, jnp.int32(chips_x))
        along_x = group - along_y * chips_x
        return (outer_at ^ (along_x * CORES)) * inner_count + (inner_at ^ along_y)

    meta = jnp.concatenate([piece[:, width:] for piece in pieces], axis=0).astype(F32)
    hit, _ = routing(meta, block_rows, capacity, groups, expert_of)
    rows = jnp.concatenate([piece[:, :width] for piece in pieces], axis=0)
    return dot_first(jnp.where(hit, 1.0, 0.0).astype(BF16), rows)


def own_kernel(sizes, *refs):
    refs[-1][...] = chosen_rows(*sizes, refs[:-1])


def select_kernel(sizes, blocks, *refs):
    own_ref, pieces, outs = refs[0], refs[1:1 + blocks], refs[2 + blocks:]
    others = chosen_rows(*sizes, pieces)
    part = others.shape[0] // len(outs)
    for at, out in enumerate(outs):
        chosen = slice(at * part, (at + 1) * part)
        out[...] = jnp.concatenate([own_ref[chosen], others[chosen]], axis=0).astype(BF16)


def hidden_kernel(width, blocks, *refs):
    pieces, (gate_ref, up_ref, _), refs = refs[:blocks], refs[blocks:blocks + 3], refs[blocks + 3:]
    copies = []
    if len(refs) > 1:
        source, refs, sem = refs[0], refs[1:-1], refs[-1]
        copies = [
            pltpu.make_async_copy(columns(source, at, target.shape[1]), target, sem.at[at - 1])
            for at, target in enumerate(refs[1:], 1)
        ]
    for copy in copies:
        copy.start()
    rows = jnp.concatenate([piece[:, :width] for piece in pieces], axis=0)
    gate = dot(rows, gate_ref[...])
    up = dot(rows, up_ref[...])
    refs[0][...] = (gate / (1.0 + jnp.exp(-gate)) * up).astype(BF16)
    for copy in copies:
        copy.wait()


def hidden(pieces, gate, up, loaded, *later):
    shapes = [(sum(piece.shape[0] for piece in pieces), gate.shape[1])]
    for array in later:
        shapes += [(array.shape[0], array.shape[1] // OUT_CUTS)] * (OUT_CUTS - 1)
    return call(
        functools.partial(hidden_kernel, gate.shape[0], len(pieces)),
        [pltpu.VMEM(shape, BF16) for shape in shapes],
        *pieces,
        near(gate),
        near(up),
        loaded,
        *[far(array) for array in later],
        in_specs=[IN_VMEM] * (len(pieces) + 2) + [ANYWHERE] * (1 + len(later)),
        out_specs=[IN_VMEM] * len(shapes),
        scratch_shapes=[pltpu.SemaphoreType.DMA((OUT_CUTS - 1,))] if later else [],
    )


def down_kernel(chips_x, depth_y, hidden_ref, down_ref, *outs):
    answer = dot(hidden_ref[...], down_ref[...])
    part = outs[0].shape[0] // depth_y
    for at, out in enumerate(outs):
        along_x, core = at // CORES, at % CORES
        firsts = [((y * chips_x + along_x) * CORES + core) * part for y in range(depth_y)]
        out[...] = jnp.concatenate([answer[first:first + part] for first in firsts], axis=0).astype(BF16)


def down(rows, matrix, outer_count, depth_y):
    return call(
        functools.partial(down_kernel, outer_count // CORES, depth_y),
        [whole((rows.shape[0] // outer_count, matrix.shape[1]), BF16)] * outer_count,
        rows,
        near(matrix),
    )


def table_kernel(width, block_rows, capacity, inner_count, group_count, blocks, *refs):
    pieces, (high_ref, low_ref) = refs[:blocks], refs[blocks:]
    outer_at, inner_at = lax.axis_index("outer"), lax.axis_index("inner")
    meta = jnp.concatenate([piece[:, width:] for piece in pieces], axis=0).astype(F32)
    hit, weight = routing(
        meta, block_rows, capacity, group_count, lambda group: (outer_at ^ group) * inner_count + inner_at
    )
    weight = jnp.where(hit, weight, 0.0)
    high = weight.astype(BF16)
    high_ref[...] = high
    low_ref[...] = (weight - high.astype(F32)).astype(BF16)


def shared_kernel(hidden_ref, down_ref, *outs):
    width = outs[0].shape[1]
    for at, out in enumerate(outs):
        out[...] = dot(hidden_ref[...], down_ref[:, at * width:(at + 1) * width])


def combine_kernel(blocks, base_ref, high_ref, low_ref, *refs):
    answers, keep_ref, outs = refs[:blocks], refs[blocks], refs[blocks + 1:]
    answers = [answers[0], answers[-1], *answers[1:-1]]
    rows = jnp.concatenate([answer[...] for answer in answers], axis=0)
    total = base_ref[...] + dot(high_ref[...], rows) + dot(low_ref[...], rows)
    each = keep_ref.shape[0]
    keep_ref[...] = total[:each]
    for at, out in enumerate(outs):
        out[...] = total[(at + 1) * each:(at + 2) * each].astype(BF16)


def combine(base, high, low, answers, sends):
    each, width = base.shape[0] // (sends + 1), base.shape[1]
    return call(
        functools.partial(combine_kernel, len(answers)),
        [whole((each, width), F32)] + [whole((each, width), BF16)] * sends,
        base,
        high,
        low,
        answers[0],
        *answers[2:],
        answers[1],
    )


def add_kernel(blocks, kept_ref, *refs):
    arrived, outs = refs[:blocks], refs[blocks:]
    total = kept_ref[...]
    for block in arrived:
        total = total + block[...].astype(F32)
    each = outs[0].shape[0]
    for at, out in enumerate(outs):
        out[...] = total[at * each:(at + 1) * each].astype(out.dtype)


def finish_kernel(blocks, width, *refs):
    out_ref = refs[-1]
    for at in range((len(refs) - 1) // blocks):
        group = refs[at * blocks:(at + 1) * blocks]
        total = group[0][...]
        for block in group[1:]:
            total = total + block[...].astype(F32)
        out_ref[:, at * width:(at + 1) * width] = total.astype(BF16)


def per_device(
    tokens,
    experts,
    gate_score,
    expert_gate,
    expert_up,
    expert_down,
    shared_gate,
    shared_up,
    shared_down,
):
    rows, model_width = tokens.shape
    inner_count = lax.axis_size("inner")
    outer_count = lax.axis_size("outer")
    depth_y = inner_count // DEPTH_Z
    chips_x = outer_count // CORES
    capacity = TOPK // TOP_GROUPS * rows // inner_count
    device_count = inner_count * outer_count

    def swap(array, distance):
        return lax.ppermute(array, BOTH, [(at, at ^ distance) for at in range(device_count)])

    def along_z(k):
        return k * depth_y

    def along_outer(k):
        return k * inner_count

    sent = prepare(tokens, experts, gate_score)
    column = [sent] + [None] * (DEPTH_Z - 1)
    for k in reversed(range(1, DEPTH_Z)):
        column[k] = swap(sent, along_z(k))
    beside = [swap(sent, k) for k in range(1, depth_y)]
    gate, up, loaded = prefetch(expert_gate[0], expert_up[0], order=sent)
    column[FIRST_Z], loaded = lax.optimization_barrier((column[FIRST_Z], loaded))
    *beside, loaded = lax.optimization_barrier((*beside, loaded))
    other = [None] * DEPTH_Z
    for k in reversed(range(DEPTH_Z)):
        other[k] = swap(column[k], along_outer(1))

    groups = depth_y * chips_x
    part = DEPTH_Z * capacity
    sizes = (model_width, rows, capacity, inner_count, chips_x, groups)
    own_rows = call(
        functools.partial(own_kernel, sizes), whole((groups * part, model_width), F32), *column
    )
    blocks = call(
        functools.partial(select_kernel, sizes, DEPTH_Z),
        [whole((CORES * part, model_width), BF16)] * groups,
        own_rows,
        *other,
        loaded,
        in_specs=[IN_VMEM] * (1 + DEPTH_Z) + [ANYWHERE],
        out_specs=[IN_VMEM] * groups,
    )
    arrived = [blocks[0]] + [None] * (groups - 1)
    for at in reversed(range(1, groups)):
        along_y, along_x = at // chips_x, at % chips_x
        arrived[at] = swap(blocks[at], along_y + along_outer(along_x * CORES))

    segment = list(column)
    for block in beside:
        block = after(block, *blocks)
        segment.append(block)
        moved = {k: swap(block, along_z(k)) for k in WAY_SHARED}
        for k, block in zip(WAY_SHARED, lax.optimization_barrier(tuple(moved.values()))):
            moved[k] = block
        segment += [moved[k] for k in range(1, DEPTH_Z)]
    *shared_weights, first_down, loaded = prefetch(
        shared_gate, shared_up, shared_down, half=expert_down[0]
    )
    way = sorted(range(groups), key=lambda at: (at % chips_x > 0, at // chips_x > 0, at))
    *coming, loaded = lax.optimization_barrier((*[arrived[at] for at in way], loaded))
    for at, block in zip(way, coming):
        arrived[at] = block
    expert_hidden, *down_weights = hidden(arrived, gate, up, loaded, expert_down[0])
    down_weights = [first_down] + down_weights
    high, low = call(
        functools.partial(
            table_kernel, model_width, rows, capacity, inner_count, outer_count, len(segment)
        ),
        [whole((rows * inner_count, device_count * capacity), BF16)] * 2,
        *segment,
        in_specs=[IN_VMEM] * len(segment),
    )
    (shared_hidden,) = hidden(segment, *shared_weights[:2], loaded)

    bases = call(
        shared_kernel,
        [whole((rows * inner_count, model_width // OUT_CUTS), F32)] * OUT_CUTS,
        shared_hidden,
        near(shared_weights[2]),
    )

    out_width = model_width // OUT_CUTS
    finals = []
    for at in range(OUT_CUTS):
        blocks = down(expert_hidden, down_weights[at], outer_count, depth_y)
        answers = [blocks[0]] + [None] * (outer_count - 1)
        for k in reversed(range(1, outer_count)):
            answers[k] = swap(blocks[k], along_outer(k))
        kept, *leaving = combine(bases[at], high, low, answers, depth_y - 1)
        coming = [swap(block, k + 1) for k, block in enumerate(leaving)]
        kept, *leaving = call(
            functools.partial(add_kernel, depth_y - 1),
            [whole((rows, out_width), F32)] + [whole((rows, out_width), BF16)] * (DEPTH_Z - 1),
            kept,
            *coming,
        )
        coming = [swap(leaving[k - 1], along_z(k)) for k in WAY_BACK]
        finals += [kept] + coming
    return call(
        functools.partial(finish_kernel, DEPTH_Z, out_width), whole((rows, model_width), BF16), *finals
    )


def solution(mesh):
    return jax.shard_map(
        per_device,
        mesh=mesh,
        in_specs=(
            P(("outer", "inner"), None),
            P(("outer", "inner"), None),
            P(("outer", "inner"), None),
            P(("outer", "inner"), None, None),
            P(("outer", "inner"), None, None),
            P(("outer", "inner"), None, None),
            P(None, "inner"),
            P(None, "inner"),
            P("inner", None),
        ),
        out_specs=P(("outer", "inner"), None),
        check_vma=False,
    )
```
